32 devices in a mesh: row: 8 (over z, core), col: 4 (over y, x).
Axes of the slice: x: 2, y: 2, z: 4, core: 2. Of those that a mesh axis runs over, the one named last changes fastest.
Arguments:
- momentum: float32 [4096, 6656], P('row', 'col'), may hold values from -20 to 20
- grad: bfloat16 [4096, 6656], P('row', 'col'), may hold values from -3 to 3
- basis: float32 [6656, 128], P('col'), may hold values from -0.078125 to 0.078125
Outputs:
- momentum_out: float32 [4096, 6656], P('row', 'col')
- left_out: float32 [2, 4096, 128], P(None, 'row')
- right_out: float32 [6656, 128], P('col')
The draws below stay inside these ranges and needn't reach their ends.
All inputs are finite; a program needn't handle non-finite values.
Results may differ from the reference program's by a relative error of at most 0.0003.
Values sent between devices are 32-bit elements; how exact they have to be, the bound alone decides.
No kernel may reach another device: no remote copies, remote signals or barrier semaphores. Data moves between devices by JAX's collectives and lax.ppermute only.
A program may use at most 64 MiB of HBM per device.

```python
import jax
import jax.numpy as jnp
from jax import lax

RANK = 128
ITERS = 2
ROWS = 4096
COLS = 6656


def draw_momentum(key, part):
    key = jax.random.fold_in(key, 7)
    keys = jax.random.split(key, 3)
    row_pos = jnp.arange(ROWS, dtype=jnp.float32) / ROWS
    col_pos = jnp.arange(COLS, dtype=jnp.float32) / COLS
    row_scale = jnp.exp(jnp.log(3.0) * row_pos) * jnp.exp(jax.random.uniform(keys[0], (ROWS,)) * jnp.log(4.0))
    col_scale = jnp.exp(jnp.log(3.0) * col_pos) * jnp.exp(jax.random.uniform(keys[1], (COLS,)) * jnp.log(4.0))
    base = jnp.clip(jax.random.normal(keys[2], (ROWS, COLS)), -4.0, 4.0)
    values = 0.3 * base * row_scale[:, None] * col_scale[None, :]
    return jnp.clip(values, -20.0, 20.0).astype(jnp.float32)


def levels(own_key, dims, cuts, least, largest):
    factor_of = 1.0
    for dim, shards_of in cuts:
        steps = jax.random.uniform(jax.random.fold_in(jax.random.fold_in(own_key, 6), dim), (shards_of,), jnp.float32, least / len(cuts), largest / len(cuts))
        factor_of = factor_of * jnp.repeat(jnp.exp(steps), dims[dim] // shards_of).reshape((-1,) + (1,) * (len(dims) - 1 - dim))
    return factor_of


def noise(stream_key, dims, width, most, cuts=(), held_as=jnp.bfloat16):
    gain = levels(stream_key, dims, cuts, -0.22, 0.18) if cuts else 1.0
    drawn = jax.random.normal(stream_key, dims, jnp.float32) * width * gain
    return jnp.minimum(jnp.maximum(drawn, -most), most).astype(held_as)


def setup_inputs(seed: int = 0) -> dict:
    seeds = jax.random.split(jax.random.key(seed), 4)
    momentum = draw_momentum(jax.random.fold_in(seeds[3], 71), 0)
    grad = noise(seeds[1], (ROWS, COLS), 0.5, 3.0, ((0, 8), (1, 4)))
    basis = noise(seeds[2], (COLS, RANK), COLS ** -0.5, 0.078125, ((0, 4),), jnp.float32)
    return {"momentum": momentum, "grad": grad, "basis": basis}


def orthonormal(proj):
    gram = jnp.dot(proj.T, proj, precision=lax.Precision.HIGHEST)
    lower = jnp.linalg.cholesky(gram)
    return jax.scipy.linalg.solve_triangular(lower, proj.T, lower=True).T

def reference(momentum, grad, basis):
    work = momentum + grad.astype(jnp.float32)
    lefts = []
    for step in range(ITERS):
        proj = jnp.dot(work, basis, precision=lax.Precision.HIGHEST)
        left = orthonormal(proj)
        right_raw = jnp.dot(work.T, left, precision=lax.Precision.HIGHEST)
        basis = orthonormal(right_raw)
        work = work - 0.95 * jnp.dot(left, right_raw.T, precision=lax.Precision.HIGHEST)
        lefts.append(left * jnp.sqrt(jnp.float32(ROWS)))
    return (work, jnp.stack(lefts), basis * jnp.sqrt(jnp.float32(COLS)))
```

```python
import jax
import jax.numpy as jnp
from jax import lax
from jax.sharding import PartitionSpec as P

ITERS = 2
HIGHEST = lax.Precision.HIGHEST
HIGH = lax.Precision.HIGH


def mm(a, b, dims, precision=HIGH):
    return lax.dot_general(a, b, ((dims[0], dims[1]), ((), ())), precision=precision)


def masks_of(axis):
    size = lax.axis_size(axis)
    masks = []
    mask = 1
    while mask < size:
        masks.append(mask)
        mask *= 2
    assert mask == size
    return masks


def swap(x, axis, mask):
    return lax.ppermute(x, axis, [(i, i ^ mask) for i in range(lax.axis_size(axis))])


def sum_whole(x, axis):
    for mask in masks_of(axis):
        x = x + swap(x, axis, mask)
    return x


def sum_halving(x, axis):
    place = lax.axis_index(axis)
    masks = masks_of(axis)
    for mask in masks:
        half = x.shape[0] // 2
        bit = (place // mask) % 2
        keep = lax.dynamic_slice_in_dim(x, bit * half, half)
        send = lax.dynamic_slice_in_dim(x, (1 - bit) * half, half)
        x = keep + swap(send, axis, mask)
    for mask in reversed(masks):
        bit = (place // mask) % 2
        other = swap(x, axis, mask)
        low = jnp.where(bit == 0, x, other)
        high = jnp.where(bit == 0, other, x)
        x = jnp.concatenate([low, high], axis=0)
    return x


def gram_of(x):
    return mm(x, x, ((0,), (0,)), HIGHEST)


def factor(gram):
    lower = jnp.linalg.cholesky(gram)
    eye = jnp.eye(gram.shape[0], dtype=gram.dtype)
    return jax.scipy.linalg.solve_triangular(lower, eye, lower=True)


def shards(momentum, grad, basis):
    work = momentum + grad.astype(jnp.float32)
    total_rows = momentum.shape[0] * lax.axis_size("row")
    total_cols = momentum.shape[1] * lax.axis_size("col")
    proj = sum_whole(mm(work, basis, ((1,), (0,))), "col")
    lefts = []
    rights = []
    for step in range(ITERS):
        gram_left = sum_whole(gram_of(proj), "row")
        partial = mm(work, proj, ((0,), (0,)))
        for left, right in zip(lefts, rights):
            partial = partial - 0.95 * mm(right, mm(left, proj, ((0,), (0,))), ((1,), (0,)))
        inv_left = factor(gram_left)
        left = mm(proj, inv_left, ((1,), (1,)), HIGHEST)
        right = mm(sum_halving(partial, "row"), inv_left, ((1,), (1,)), HIGHEST)
        lefts.append(left)
        rights.append(right)
        gram_right = sum_whole(gram_of(right), "col")
        inv_right = factor(gram_right)
        if step + 1 < ITERS:
            image = sum_whole(mm(work, right, ((1,), (0,))), "col")
            for other_left, other_right in zip(lefts[:-1], rights[:-1]):
                cross = lax.psum(mm(other_right, right, ((0,), (0,))), "col")
                image = image - 0.95 * mm(other_left, cross, ((1,), (0,)))
            image = image - 0.95 * mm(left, gram_right, ((1,), (0,)), HIGHEST)
            proj = mm(image, inv_right, ((1,), (1,)), HIGHEST)
    basis_out = mm(rights[-1], inv_right, ((1,), (1,)), HIGHEST)
    outer = mm(jnp.concatenate(lefts, axis=1), jnp.concatenate(rights, axis=1), ((1,), (1,)))
    return (
        work - 0.95 * outer,
        jnp.stack(lefts) * jnp.sqrt(jnp.float32(total_rows)),
        basis_out * jnp.sqrt(jnp.float32(total_cols)),
    )


def solution(mesh):
    in_specs = (P("row", "col"), P("row", "col"), P("col", None))
    out_specs = (P("row", "col"), P(None, "row", None), P("col", None))
    return jax.shard_map(shards, mesh=mesh, in_specs=in_specs, out_specs=out_specs, check_vma=False)
```

```python
import jax
import jax.numpy as jnp
from jax import lax
from jax.experimental import pallas as pl
from jax.experimental.pallas import tpu as pltpu
from jax.sharding import PartitionSpec as P

ITERS = 2
HIGHEST = lax.Precision.HIGHEST
HIGH = lax.Precision.HIGH


def mm(a, b, dims, precision=HIGH):
    return lax.dot_general(a, b, ((dims[0], dims[1]), ((), ())), precision=precision)


def masks_of(axis):
    size = lax.axis_size(axis)
    masks = []
    mask = 1
    while mask < size:
        masks.append(mask)
        mask *= 2
    assert mask == size
    return masks


def swap(x, axis, mask):
    return lax.ppermute(x, axis, [(i, i ^ mask) for i in range(lax.axis_size(axis))])


def sum_whole(x, axis):
    for mask in masks_of(axis):
        x = x + swap(x, axis, mask)
    return x


def sum_halving(x, axis):
    place = lax.axis_index(axis)
    masks = masks_of(axis)
    for mask in masks:
        half = x.shape[0] // 2
        bit = (place // mask) % 2
        keep = lax.dynamic_slice_in_dim(x, bit * half, half)
        send = lax.dynamic_slice_in_dim(x, (1 - bit) * half, half)
        x = keep + swap(send, axis, mask)
    for mask in reversed(masks):
        bit = (place // mask) % 2
        other = swap(x, axis, mask)
        low = jnp.where(bit == 0, x, other)
        high = jnp.where(bit == 0, other, x)
        x = jnp.concatenate([low, high], axis=0)
    return x


def gram_of(x):
    return mm(x, x, ((0,), (0,)), HIGHEST)


def eliminate(full, first):
    rank = full.shape[1]
    sub = lax.broadcasted_iota(jnp.int32, (8, rank), 0)
    lane = lax.broadcasted_iota(jnp.int32, (8, rank), 1)
    rolled = pltpu.roll(full, lax.rem(rank - first, rank), 1)
    cols = [jnp.broadcast_to(rolled[:, j:j + 1], (8, rank)) for j in range(8)]
    for j in range(8):
        pivot = jnp.broadcast_to(cols[j][j:j + 1], (8, rank))
        mult = jnp.where(sub > j, cols[j] * (1.0 / pivot), 0.0)
        for k in range(j + 1, 8):
            cols[k] = cols[k] - mult * cols[k][j:j + 1]
        here = lane == first + j
        row = jnp.where(here[:1], 1.0, full[j:j + 1])
        rest = jnp.where(here & (sub > j), 0.0, full) - mult * row
        full = jnp.where(sub == j, row * lax.rsqrt(pivot), rest)
    return full

def factor_body(gram_ref, out_ref):
    rank = gram_ref.shape[0]
    out_ref[...] = gram_ref[...]
    row = lax.broadcasted_iota(jnp.int32, (rank, rank), 0)
    col = lax.broadcasted_iota(jnp.int32, (rank, rank), 1)

    def panel(p, carry):
        first = pl.multiple_of(p * 8, 8)
        done = eliminate(out_ref[pl.ds(first, 8), :], first)
        sub = lax.broadcasted_iota(jnp.int32, (8, rank), 0)
        lane = lax.broadcasted_iota(jnp.int32, (8, rank), 1)
        lower = jnp.where((lane > first + sub) & (lane < first + 8), 0.0, done)
        step = lax.dot_general(done, lower, (((0,), (0,)), ((), ())), precision=HIGHEST, preferred_element_type=jnp.float32)
        old = out_ref[...]
        old = jnp.where(row >= first + 8, jnp.where((col >= first) & (col < first + 8), 0.0, old) - step, old)
        out_ref[...] = old
        out_ref[pl.ds(first, 8), :] = done
        return carry

    lax.fori_loop(0, rank // 8, panel, 0)
    out_ref[...] = jnp.where(row >= col, out_ref[...], 0.0)

def factor(gram):
    return pl.pallas_call(
        factor_body,
        out_shape=jax.ShapeDtypeStruct(gram.shape, gram.dtype),
        in_specs=[pl.BlockSpec(memory_space=pltpu.VMEM)],
        out_specs=pl.BlockSpec(memory_space=pltpu.VMEM),
        name="factor",
        cost_estimate=pl.CostEstimate(flops=40_000_000, bytes_accessed=131072, transcendentals=0),
    )(gram)


def shards(momentum, grad, basis):
    work = momentum + grad.astype(jnp.float32)
    total_rows = momentum.shape[0] * lax.axis_size("row")
    total_cols = momentum.shape[1] * lax.axis_size("col")
    proj = sum_whole(mm(work, basis, ((1,), (0,))), "col")
    lefts = []
    rights = []
    for step in range(ITERS):
        gram_left = sum_whole(gram_of(proj), "row")
        partial = mm(work, proj, ((0,), (0,)))
        for left, right in zip(lefts, rights):
            partial = partial - 0.95 * mm(right, mm(left, proj, ((0,), (0,))), ((1,), (0,)))
        inv_left = factor(gram_left)
        left = mm(proj, inv_left, ((1,), (1,)), HIGHEST)
        right = mm(sum_halving(partial, "row"), inv_left, ((1,), (1,)), HIGHEST)
        lefts.append(left)
        rights.append(right)
        gram_right = sum_whole(gram_of(right), "col")
        inv_right = factor(gram_right)
        if step + 1 < ITERS:
            image = sum_whole(mm(work, right, ((1,), (0,))), "col")
            for other_left, other_right in zip(lefts[:-1], rights[:-1]):
                cross = sum_whole(mm(other_right, right, ((0,), (0,))), "col")
                image = image - 0.95 * mm(other_left, cross, ((1,), (0,)))
            image = image - 0.95 * mm(left, gram_right, ((1,), (0,)), HIGHEST)
            proj = mm(image, inv_right, ((1,), (1,)), HIGHEST)
    basis_out = mm(rights[-1], inv_right, ((1,), (1,)), HIGHEST)
    outer = mm(jnp.concatenate(lefts, axis=1), jnp.concatenate(rights, axis=1), ((1,), (1,)))
    return (
        work - 0.95 * outer,
        jnp.stack(lefts) * jnp.sqrt(jnp.float32(total_rows)),
        basis_out * jnp.sqrt(jnp.float32(total_cols)),
    )


def solution(mesh):
    in_specs = (P("row", "col"), P("row", "col"), P("col", None))
    out_specs = (P("row", "col"), P(None, "row", None), P("col", None))
    return jax.shard_map(shards, mesh=mesh, in_specs=in_specs, out_specs=out_specs, check_vma=False)
```

```python
import jax
import jax.numpy as jnp
from jax import lax
from jax.experimental import pallas as pl
from jax.experimental.pallas import tpu as pltpu
from jax.sharding import PartitionSpec as P

F32 = jnp.float32
BF16 = jnp.bfloat16
HIGHEST = lax.Precision.HIGHEST
VMEM = pl.BlockSpec(memory_space=pltpu.VMEM)
SMEM = pl.BlockSpec(memory_space=pltpu.SMEM)
NN = (((1,), (0,)), ((), ()))
NT = (((1,), (1,)), ((), ()))
KEEP = 0.95


def masks_of(axis):
    size = lax.axis_size(axis)
    masks = []
    mask = 1
    while mask < size:
        masks.append(mask)
        mask *= 2
    assert mask == size
    return masks


def swap(x, axis, mask):
    return lax.ppermute(x, axis, [(i, i ^ mask) for i in range(lax.axis_size(axis))])


def sum_whole(x, axis):
    for mask in masks_of(axis):
        x = x + swap(x, axis, mask)
    return x


def split(x):
    high = x.astype(BF16)
    return high, (x - high.astype(F32)).astype(BF16)


def dot(a, b, dims=NN):
    return lax.dot_general(a, b, dims, preferred_element_type=F32)


def exact(a, b, dims=NN):
    return lax.dot_general(a, b, dims, precision=HIGHEST, preferred_element_type=F32)


def tiles(width, most=256):
    return [(start, min(most, width - start)) for start in range(0, width, most)]


def struct(*shape, dtype=F32):
    return jax.ShapeDtypeStruct(shape, dtype)


def call(body, name, out, ins, scratch=(), flops=0, nbytes=0, **kw):
    return pl.pallas_call(
        body,
        out_shape=out,
        in_specs=[SMEM if x.dtype == jnp.int32 else VMEM for x in ins],
        out_specs=jax.tree.map(lambda _: VMEM, out),
        scratch_shapes=list(scratch),
        name=name,
        compiler_params=pltpu.CompilerParams(vmem_limit_bytes=24 * 2**20),
        cost_estimate=pl.CostEstimate(flops=flops, bytes_accessed=nbytes, transcendentals=0),
        **kw,
    )(*ins)


def start_body(momentum_ref, grad_ref, basis_ref, high_ref, low_ref, top_ref, bottom_ref, both_ref):
    step = pl.program_id(0)
    rank = basis_ref.shape[1]
    rows = momentum_ref.shape[0]
    half = top_ref.shape[0] // rows

    @pl.when(step == 0)
    def _():
        high, low = split(basis_ref[...])
        both_ref[:, :rank] = high
        both_ref[:, rank:] = low

    high, low = split(momentum_ref[...] + grad_ref[...].astype(F32))
    high_ref[...] = high
    low_ref[...] = low
    wide = dot(high, both_ref[...])
    proj = wide[:, :rank] + wide[:, rank:] + dot(low, both_ref[:, :rank])

    @pl.when(step < half)
    def _():
        top_ref[pl.ds(pl.multiple_of(step * rows, rows), rows), :] = proj

    @pl.when(step >= half)
    def _():
        bottom_ref[pl.ds(pl.multiple_of((step - half) * rows, rows), rows), :] = proj


def start(momentum, grad, basis):
    rows, cols = momentum.shape
    rank = basis.shape[1]
    block = rows // 4
    tile = pl.BlockSpec((block, cols), lambda i: (i, 0))
    whole = pl.BlockSpec((rows // 2, rank), lambda i: (0, 0))
    return pl.pallas_call(
        start_body,
        grid=(4,),
        in_specs=[tile, tile, pl.BlockSpec((cols, rank), lambda i: (0, 0))],
        out_specs=[tile, tile, whole, whole],
        out_shape=[struct(rows, cols, dtype=BF16)] * 2 + [struct(rows // 2, rank)] * 2,
        scratch_shapes=[pltpu.VMEM((cols, 2 * rank), BF16)],
        name="start",
        compiler_params=pltpu.CompilerParams(vmem_limit_bytes=24 * 2**20),
    )(momentum, grad, basis)


def pull_core(place_ref, proj, high_ref, low_ref, gram_ref, keep_ref, send_ref, turned_ref, extra=None):
    rank = proj.shape[1]
    width = high_ref.shape[1]
    turned = proj.T
    gram_ref[...] = exact(turned, proj)
    turned_ref[...] = turned
    place = place_ref[0]
    half = keep_ref.shape[0]
    count = extra[0]
    chunk = rank // count
    order = [j for j in range(count) if j % 2 == 0] + [j for j in range(count) if j % 2 == 1]
    parts = [turned_ref[pl.ds(pl.multiple_of((place ^ j) * chunk, chunk), chunk), :] for j in order]
    turned = jnp.concatenate(parts, axis=0)
    high, low = split(turned)
    both = jnp.concatenate([high, low], axis=0)
    if len(extra) > 1:
        left_ref, right_ref = extra[1:]
        cross_high, cross_low = split(-KEEP * exact(turned, left_ref[...]))
        cross = jnp.concatenate([cross_high, cross_low], axis=0)
    for at, size in tiles(width):
        wide = dot(both, high_ref[:, at:at + size])
        out = wide[:rank] + wide[rank:] + dot(high, low_ref[:, at:at + size])
        if len(extra) > 1:
            right_high, right_low = split(right_ref[:, at:at + size])
            wide = dot(cross, right_high)
            out = out + (wide[:rank] + wide[rank:] + dot(cross_high, right_low))
        keep_ref[:, at:at + size] = out[:half]
        send_ref[:, at:at + size] = out[half:]


def pull(count, place, halves, high, low, before=None):
    rows, width = high.shape
    rank = halves[0].shape[1]

    def body(place_ref, a, b, c, d, high_ref, low_ref, *rest):
        total = jnp.concatenate([a[...] + b[...], c[...] + d[...]], axis=0)
        if before is None:
            proj_ref, gram_ref, keep_ref, send_ref, turned_ref = rest
            extra = (count,)
        else:
            left_ref, right_ref, gram_in, inv_ref, proj_ref, gram_ref, keep_ref, send_ref, turned_ref = rest
            total = total - KEEP * exact(left_ref[...], gram_in[...])
            total = exact(total, inv_ref[...], NT)
            extra = (count, left_ref, right_ref)
        proj_ref[...] = total
        pull_core(place_ref, total, high_ref, low_ref, gram_ref, keep_ref, send_ref, turned_ref, extra)

    out = [struct(rows, rank), struct(rank, rank), struct(rank // 2, width), struct(rank // 2, width)]
    ins = [place, *halves, high, low] + list(before or [])
    return call(body, "pull", out, ins, [pltpu.VMEM((rank, rows), F32)], flops=1_000_000_000, nbytes=5_000_000)


def push_body(count, last, place_ref, inv_ref, proj_ref, high_ref, low_ref, *rest):
    pieces = rest[:count]
    if last:
        left_ref, right_ref, gram_ref, raw_ref = rest[count:]
    else:
        left_ref, right_ref, gram_ref, top_ref, bottom_ref, raw_ref = rest[count:]
    rank, width = right_ref.shape
    chunk = rank // count
    place = place_ref[0]
    for j, piece in enumerate(pieces):
        raw_ref[pl.ds(pl.multiple_of((place ^ j) * chunk, chunk), chunk), :] = piece[...]
    inv = inv_ref[...]
    inv_high, inv_low = split(inv)
    inv_both = jnp.concatenate([inv_high, inv_low], axis=0)
    gram = jnp.zeros((rank, rank), F32)
    image = None
    for at, size in tiles(width):
        raw_high, raw_low = split(raw_ref[:, at:at + size])
        wide = dot(inv_both, raw_high)
        right = wide[:rank] + wide[rank:] + dot(inv_high, raw_low)
        right_ref[:, at:at + size] = right
        high, low = split(right)
        both = jnp.concatenate([high, low], axis=0)
        wide = dot(both, high, NT)
        gram = gram + (wide[:rank] + wide[rank:] + dot(high, low, NT))
        if not last:
            wide = dot(high_ref[:, at:at + size], both, NT)
            part = wide[:, :rank] + wide[:, rank:] + dot(low_ref[:, at:at + size], high, NT)
            image = part if image is None else image + part
    gram_ref[...] = gram
    if not last:
        half = top_ref.shape[0]
        top_ref[...] = image[:half]
        bottom_ref[...] = image[half:]
    left_ref[...] = exact(proj_ref[...], inv, NT)


def push(count, place, inv, proj, high, low, pieces, last):
    rows, width = high.shape
    rank = inv.shape[0]
    out = [struct(rows, rank), struct(rank, width), struct(rank, rank)]
    if not last:
        out += [struct(rows // 2, rank)] * 2

    def body(*refs):
        push_body(count, last, *refs)

    ins = [place, inv, proj, high, low, *pieces]
    return call(body, "push", out, ins, [pltpu.VMEM((rank, width), F32)], flops=1_000_000_000, nbytes=5_000_000)


def finish_body(scale, momentum_ref, grad_ref, left_a, left_b, right_a, right_b, out_ref, lefts_ref, high_ref, low_ref):
    rank, width = right_a.shape

    @pl.when(pl.program_id(0) == 0)
    def _():
        for i, ref in enumerate((right_a, right_b)):
            high, low = split(KEEP * ref[...])
            high_ref[i * rank:(i + 1) * rank, :] = high
            low_ref[i * rank:(i + 1) * rank, :] = low

    lefts_ref[0] = scale * left_a[...]
    lefts_ref[1] = scale * left_b[...]
    high, low = split(jnp.concatenate([left_a[...], left_b[...]], axis=1))
    for at, size in tiles(width):
        right_high = high_ref[:, at:at + size]
        outer = dot(high, right_high) + dot(low, right_high) + dot(high, low_ref[:, at:at + size])
        work = momentum_ref[:, at:at + size] + grad_ref[:, at:at + size].astype(F32)
        out_ref[:, at:at + size] = work - outer


def finish(momentum, grad, left_a, left_b, right_a, right_b, scale):
    rows, cols = momentum.shape
    rank = left_a.shape[1]
    block = rows // 4
    tile = pl.BlockSpec((block, cols), lambda i: (i, 0))
    left_tile = pl.BlockSpec((block, rank), lambda i: (i, 0))
    right_tile = pl.BlockSpec((rank, cols), lambda i: (0, 0))

    def body(*refs):
        finish_body(scale, *refs)

    return pl.pallas_call(
        body,
        grid=(4,),
        in_specs=[tile, tile, left_tile, left_tile, right_tile, right_tile],
        out_specs=[tile, pl.BlockSpec((2, block, rank), lambda i: (0, i, 0))],
        out_shape=[struct(rows, cols), struct(2, rows, rank)],
        scratch_shapes=[pltpu.VMEM((2 * rank, cols), BF16)] * 2,
        name="finish",
        compiler_params=pltpu.CompilerParams(vmem_limit_bytes=24 * 2**20),
        cost_estimate=pl.CostEstimate(flops=1_500_000_000, bytes_accessed=12_000_000, transcendentals=0),
    )(momentum, grad, left_a, left_b, right_a, right_b)


def eliminate(full, first):
    rank = full.shape[1]
    sub = lax.broadcasted_iota(jnp.int32, (8, rank), 0)
    lane = lax.broadcasted_iota(jnp.int32, (8, rank), 1)
    rolled = pltpu.roll(full, lax.rem(rank - first, rank), 1)
    cols = [jnp.broadcast_to(rolled[:, j:j + 1], (8, rank)) for j in range(8)]
    for j in range(8):
        pivot = jnp.broadcast_to(cols[j][j:j + 1], (8, rank))
        mult = jnp.where(sub > j, cols[j] * (1.0 / pivot), 0.0)
        for k in range(j + 1, 8):
            cols[k] = cols[k] - mult * cols[k][j:j + 1]
        here = lane == first + j
        row = jnp.where(here[:1], 1.0, full[j:j + 1])
        rest = jnp.where(here & (sub > j), 0.0, full) - mult * row
        full = jnp.where(sub == j, row * lax.rsqrt(pivot), rest)
    return full

def factor_body(gram_ref, out_ref):
    rank = gram_ref.shape[0]
    out_ref[...] = gram_ref[...]
    row = lax.broadcasted_iota(jnp.int32, (rank, rank), 0)
    col = lax.broadcasted_iota(jnp.int32, (rank, rank), 1)

    def panel(p, carry):
        first = pl.multiple_of(p * 8, 8)
        done = eliminate(out_ref[pl.ds(first, 8), :], first)
        sub = lax.broadcasted_iota(jnp.int32, (8, rank), 0)
        lane = lax.broadcasted_iota(jnp.int32, (8, rank), 1)
        lower = jnp.where((lane > first + sub) & (lane < first + 8), 0.0, done)
        step = lax.dot_general(done, lower, (((0,), (0,)), ((), ())), precision=HIGHEST, preferred_element_type=jnp.float32)
        old = out_ref[...]
        old = jnp.where(row >= first + 8, jnp.where((col >= first) & (col < first + 8), 0.0, old) - step, old)
        out_ref[...] = old
        out_ref[pl.ds(first, 8), :] = done
        return carry

    lax.fori_loop(0, rank // 8, panel, 0)
    out_ref[...] = jnp.where(row >= col, out_ref[...], 0.0)

def factor(gram):
    return call(factor_body, "factor", struct(*gram.shape), [gram], flops=2_000_000_000, nbytes=131072)


def last_factor(gram, right, scale):
    def body(gram_ref, right_ref, out_ref, inv_ref):
        factor_body(gram_ref, inv_ref)
        turned = right_ref[...].T
        high, low = split(turned)
        inv_high, inv_low = split(scale * inv_ref[...])
        both = jnp.concatenate([inv_high, inv_low], axis=0)
        rank = inv_high.shape[0]
        wide = dot(high, both, NT)
        out_ref[...] = wide[:, :rank] + wide[:, rank:] + dot(low, inv_high, NT)

    rank, width = right.shape
    return call(body, "last_factor", struct(width, rank), [gram, right], [pltpu.VMEM((rank, rank), F32)],
                flops=2_000_000_000, nbytes=2_000_000)


def sum_halves(top, bottom, axis):
    masks = masks_of(axis)
    for one, two in zip(masks[:-1], masks[:0:-1]):
        other_top, other_bottom = swap(top, axis, one), swap(bottom, axis, two)
        top, bottom = top + other_top, bottom + other_bottom
    return top, swap(top, axis, masks[-1]), bottom, swap(bottom, axis, masks[0])


def sum_rows(keep, send, count):
    rows = 2 * keep.shape[0] // count
    keep = keep + swap(send, "row", 1)
    chunks = [keep[i * rows:(i + 1) * rows] for i in range(count // 2)]
    own = chunks[0]
    for i in range(1, count // 2):
        own = own + swap(chunks[i], "row", 2 * i)
    even = [own] + [swap(own, "row", 2 * i) for i in range(1, count // 2)]
    odd = [swap(x, "row", 1) for x in even]
    return [x for pair in zip(even, odd) for x in pair]


def shards(momentum, grad, basis):
    count = lax.axis_size("row")
    row_scale = float(momentum.shape[0] * count) ** 0.5
    col_scale = float(momentum.shape[1] * lax.axis_size("col")) ** 0.5
    place = lax.axis_index("row").astype(jnp.int32).reshape(1)
    high, low, top, bottom = start(momentum, grad, basis)
    halves = sum_halves(top, bottom, "col")
    proj, gram, keep, send = pull(count, place, halves, high, low)
    inv = factor(sum_whole(gram, "row"))
    pieces = sum_rows(keep, send, count)
    left_a, right_a, gram, top, bottom = push(count, place, inv, proj, high, low, pieces, False)
    gram = sum_whole(gram, "col")
    halves = sum_halves(top, bottom, "col")
    inv = factor(gram)
    proj, gram, keep, send = pull(count, place, halves, high, low, (left_a, right_a, gram, inv))
    inv = factor(sum_whole(gram, "row"))
    pieces = sum_rows(keep, send, count)
    left_b, right_b, gram = push(count, place, inv, proj, high, low, pieces, True)
    gram = sum_whole(gram, "col")
    momentum_out, lefts = finish(momentum, grad, left_a, left_b, right_a, right_b, row_scale)
    return momentum_out, lefts, last_factor(gram, right_b, col_scale)


def solution(mesh):
    in_specs = (P("row", "col"), P("row", "col"), P("col", None))
    out_specs = (P("row", "col"), P(None, "row", None), P("col", None))
    return jax.shard_map(shards, mesh=mesh, in_specs=in_specs, out_specs=out_specs, check_vma=False)
```

```python
import jax
import jax.numpy as jnp
from jax import lax
from jax.experimental import pallas as pl
from jax.experimental.pallas import tpu as pltpu
from jax.sharding import PartitionSpec as P

F32 = jnp.float32
BF16 = jnp.bfloat16
HIGHEST = lax.Precision.HIGHEST
VMEM = pl.BlockSpec(memory_space=pltpu.VMEM)
SMEM = pl.BlockSpec(memory_space=pltpu.SMEM)
NN = (((1,), (0,)), ((), ()))
NT = (((1,), (1,)), ((), ()))
TN = (((0,), (0,)), ((), ()))
KEEP = 0.95
PANEL = 16
FACTOR = 1_500_000_000


def masks_of(axis):
    size = lax.axis_size(axis)
    masks = []
    mask = 1
    while mask < size:
        masks.append(mask)
        mask *= 2
    assert mask == size
    return masks


def swap(x, axis, mask):
    return lax.ppermute(x, axis, [(i, i ^ mask) for i in range(lax.axis_size(axis))])


def sum_part(x, axis):
    masks = masks_of(axis)
    for mask in masks[:-1]:
        x = x + swap(x, axis, mask)
    return x, swap(x, axis, masks[-1])


def split(x):
    high = x.astype(BF16)
    return high, (x - high.astype(F32)).astype(BF16)


def dot(a, b, dims=NN):
    return lax.dot_general(a, b, dims, preferred_element_type=F32)


def exact(a, b, dims=NN):
    return lax.dot_general(a, b, dims, precision=HIGHEST, preferred_element_type=F32)


def tiles(width, most=256):
    return [(start, min(most, width - start)) for start in range(0, width, most)]


def struct(*shape, dtype=F32):
    return jax.ShapeDtypeStruct(shape, dtype)


def call(body, name, out, ins, scratch=(), flops=0, nbytes=0, **kw):
    return pl.pallas_call(
        body,
        out_shape=out,
        in_specs=[SMEM if x.dtype == jnp.int32 else VMEM for x in ins],
        out_specs=jax.tree.map(lambda _: VMEM, out),
        scratch_shapes=list(scratch),
        name=name,
        compiler_params=pltpu.CompilerParams(vmem_limit_bytes=24 * 2**20),
        cost_estimate=pl.CostEstimate(flops=flops, bytes_accessed=nbytes, transcendentals=0),
        **kw,
    )(*ins)


def start_body(momentum_ref, grad_ref, basis_ref, high_ref, low_ref, top_ref, bottom_ref, both_ref):
    step = pl.program_id(0)
    rank = basis_ref.shape[1]
    rows = momentum_ref.shape[0]
    half = top_ref.shape[0] // rows

    @pl.when(step == 0)
    def _():
        high, low = split(basis_ref[...])
        both_ref[:, :rank] = high
        both_ref[:, rank:] = low

    high, low = split(momentum_ref[...] + grad_ref[...].astype(F32))
    high_ref[...] = high
    low_ref[...] = low
    wide = dot(high, both_ref[...])
    proj = wide[:, :rank] + wide[:, rank:] + dot(low, both_ref[:, :rank])

    @pl.when(step < half)
    def _():
        top_ref[pl.ds(pl.multiple_of(step * rows, rows), rows), :] = proj

    @pl.when(step >= half)
    def _():
        bottom_ref[pl.ds(pl.multiple_of((step - half) * rows, rows), rows), :] = proj


def start(momentum, grad, basis):
    rows, cols = momentum.shape
    rank = basis.shape[1]
    block = rows // 4
    tile = pl.BlockSpec((block, cols), lambda i: (i, 0))
    whole = pl.BlockSpec((rows // 2, rank), lambda i: (0, 0))
    return pl.pallas_call(
        start_body,
        grid=(4,),
        in_specs=[tile, tile, pl.BlockSpec((cols, rank), lambda i: (0, 0))],
        out_specs=[tile, tile, whole, whole],
        out_shape=[struct(rows, cols, dtype=BF16)] * 2 + [struct(rows // 2, rank)] * 2,
        scratch_shapes=[pltpu.VMEM((cols, 2 * rank), BF16)],
        name="start",
        compiler_params=pltpu.CompilerParams(vmem_limit_bytes=24 * 2**20),
    )(momentum, grad, basis)


def pull(count, place, halves, high, low, before=None):
    rows, width = high.shape
    rank = halves[0].shape[1]
    chunk = rank // count
    order = [*range(0, count, 2), *range(1, count, 2)]

    def body(place_ref, a, b, c, d, high_ref, low_ref, *rest):
        proj = jnp.concatenate([a[...] + b[...], c[...] + d[...]], axis=0)
        if before is None:
            proj_ref, keep_ref, send_ref, turned_ref = rest
        else:
            left_ref, right_ref, gram_ref, inv_ref, proj_ref, keep_ref, send_ref, turned_ref = rest
            proj = proj - KEEP * exact(left_ref[...], gram_ref[...])
            proj = exact(proj, inv_ref[...], NT)
        proj_ref[...] = proj
        turned_ref[...] = proj.T
        place = place_ref[0]
        parts = [turned_ref[pl.ds(pl.multiple_of((place ^ j) * chunk, chunk), chunk), :] for j in order]
        turned = jnp.concatenate(parts, axis=0)
        gram = exact(turned, proj)
        half = rank // 2
        keep_ref[:, width:] = gram[:half]
        send_ref[:, width:] = gram[half:]
        high, low = split(turned)
        both = jnp.concatenate([high, low], axis=0)
        if before is not None:
            cross_high, cross_low = split(-KEEP * exact(turned, left_ref[...]))
            cross = jnp.concatenate([cross_high, cross_low], axis=0)
        for at, size in tiles(width):
            wide = dot(both, high_ref[:, at:at + size])
            out = wide[:rank] + wide[rank:] + dot(high, low_ref[:, at:at + size])
            if before is not None:
                right_high, right_low = split(right_ref[:, at:at + size])
                wide = dot(cross, right_high)
                out = out + (wide[:rank] + wide[rank:] + dot(cross_high, right_low))
            keep_ref[:, at:at + size] = out[:half]
            send_ref[:, at:at + size] = out[half:]

    out = [struct(rows, rank), struct(rank // 2, width + rank), struct(rank // 2, width + rank)]
    ins = [place, *halves, high, low] + list(before or [])
    return call(body, "pull", out, ins, [pltpu.VMEM((rank, rows), F32)], flops=1_000_000_000, nbytes=5_000_000)


def normal(count, place, inv, pieces, width):
    rank = inv.shape[0]
    chunk = rank // count

    def body(place_ref, inv_ref, *rest):
        right_ref, gram_ref, raw_ref = rest[len(pieces):]
        place = place_ref[0]
        for (lane, order, _), piece in zip(pieces, rest):
            size = piece.shape[1]
            for i, j in enumerate(order):
                rows = pl.ds(pl.multiple_of((place ^ j) * chunk, chunk), chunk)
                raw_ref[rows, lane:lane + size] = piece[i * chunk:(i + 1) * chunk, :]
        inv_high, inv_low = split(inv_ref[...])
        inv_both = jnp.concatenate([inv_high, inv_low], axis=0)
        gram = jnp.zeros((rank, rank), F32)
        for at, size in tiles(width):
            raw_high, raw_low = split(raw_ref[:, at:at + size])
            wide = dot(inv_both, raw_high)
            right = wide[:rank] + wide[rank:] + dot(inv_high, raw_low)
            right_ref[:, at:at + size] = right
            high, low = split(right)
            wide = dot(jnp.concatenate([high, low], axis=0), high, NT)
            gram = gram + (wide[:rank] + wide[rank:] + dot(high, low, NT))
        gram_ref[...] = gram

    ins = [place, inv, *(piece for _, _, piece in pieces)]
    return call(body, "normal", [struct(rank, width), struct(rank, rank)], ins, [pltpu.VMEM((rank, width), F32)],
                flops=500_000_000, nbytes=2_000_000)


def push(inv, proj, high, low, right):
    rows, width = high.shape
    rank = inv.shape[0]

    def body(inv_ref, proj_ref, high_ref, low_ref, right_ref, left_ref, top_ref, bottom_ref):
        image = None
        for at, size in tiles(width):
            right_high, right_low = split(right_ref[:, at:at + size])
            wide = dot(high_ref[:, at:at + size], jnp.concatenate([right_high, right_low], axis=0), NT)
            part = wide[:, :rank] + wide[:, rank:] + dot(low_ref[:, at:at + size], right_high, NT)
            image = part if image is None else image + part
        top_ref[...] = image[:rows // 2]
        bottom_ref[...] = image[rows // 2:]
        left_ref[...] = exact(proj_ref[...], inv_ref[...], NT)

    out = [struct(rows, rank)] + [struct(rows // 2, rank)] * 2
    return call(body, "push", out, [inv, proj, high, low, right], flops=700_000_000, nbytes=5_000_000)


def finish_body(scale, momentum_ref, grad_ref, left_a, proj_b, inv_b, right_a, right_b, out_ref, lefts_ref, high_ref, low_ref):
    rank, width = right_a.shape
    left_b = exact(proj_b[...], inv_b[...], NT)

    @pl.when(pl.program_id(0) == 0)
    def _():
        for i, ref in enumerate((right_a, right_b)):
            high, low = split(KEEP * ref[...])
            high_ref[i * rank:(i + 1) * rank, :] = high
            low_ref[i * rank:(i + 1) * rank, :] = low

    lefts_ref[0] = scale * left_a[...]
    lefts_ref[1] = scale * left_b
    high, low = split(jnp.concatenate([left_a[...], left_b], axis=1))
    for at, size in tiles(width):
        right_high = high_ref[:, at:at + size]
        outer = dot(high, right_high) + dot(low, right_high) + dot(high, low_ref[:, at:at + size])
        work = momentum_ref[:, at:at + size] + grad_ref[:, at:at + size].astype(F32)
        out_ref[:, at:at + size] = work - outer


def finish(momentum, grad, left_a, proj_b, inv_b, right_a, right_b, scale):
    rows, cols = momentum.shape
    rank = left_a.shape[1]
    block = rows // 4
    tile = pl.BlockSpec((block, cols), lambda i: (i, 0))
    left_tile = pl.BlockSpec((block, rank), lambda i: (i, 0))
    right_tile = pl.BlockSpec((rank, cols), lambda i: (0, 0))

    def body(*refs):
        finish_body(scale, *refs)

    return pl.pallas_call(
        body,
        grid=(4,),
        in_specs=[tile, tile, left_tile, left_tile, pl.BlockSpec((rank, rank), lambda i: (0, 0)), right_tile, right_tile],
        out_specs=[tile, pl.BlockSpec((2, block, rank), lambda i: (0, i, 0))],
        out_shape=[struct(rows, cols), struct(2, rows, rank)],
        scratch_shapes=[pltpu.VMEM((2 * rank, cols), BF16)] * 2,
        name="finish",
        compiler_params=pltpu.CompilerParams(vmem_limit_bytes=24 * 2**20),
        cost_estimate=pl.CostEstimate(flops=1_500_000_000, bytes_accessed=12_000_000, transcendentals=0),
    )(momentum, grad, left_a, proj_b, inv_b, right_a, right_b)


def eliminate(full, first):
    rank = full.shape[1]
    groups = PANEL // 8
    sub = lax.broadcasted_iota(jnp.int32, (8, rank), 0)
    lane = lax.broadcasted_iota(jnp.int32, (8, rank), 1)
    rolled = pltpu.roll(full, lax.rem(rank - first, rank), 1)
    rows = [full[8 * g:8 * g + 8] for g in range(groups)]
    cols = [
        [jnp.broadcast_to(rolled[8 * g:8 * g + 8, j:j + 1], (8, rank)) for g in range(groups)] for j in range(PANEL)
    ]

    def spread(x, j):
        return jnp.broadcast_to(x[j // 8][j % 8:j % 8 + 1], (8, rank))

    pivot = spread(cols[0], 0)
    for j in range(PANEL):
        at = j // 8
        root = lax.rsqrt(pivot)
        if j + 1 < PANEL:
            above = spread(cols[j + 1], j) * root
            pivot = spread(cols[j + 1], j + 1) - above * above
        below = sub > j % 8
        here = lane == first + j
        row = jnp.where(here, 1.0, spread(rows, j)) * root
        for g in range(at, groups):
            mult = cols[j][g] * root
            rest = jnp.where(here, 0.0, rows[g])
            if g == at:
                mult = jnp.where(below, mult, 0.0)
                rest = jnp.where(below, rest, rows[g])
            rest = rest - mult * row
            rows[g] = jnp.where(sub == j % 8, row, rest) if g == at else rest
            cols[j][g] = mult
        for k in range(j + 1, PANEL):
            across = spread(cols[k], j) * root
            for g in range(at, groups):
                cols[k][g] = cols[k][g] - cols[j][g] * across
    return jnp.concatenate(rows, axis=0)


def thirds(x):
    high = x.astype(BF16)
    rest = x - high.astype(F32)
    middle = rest.astype(BF16)
    return high, middle, (rest - middle.astype(F32)).astype(BF16)


def factor_panels(state_ref, begin, end):
    rank = state_ref.shape[0]
    row = lax.broadcasted_iota(jnp.int32, (rank, rank), 0)
    col = lax.broadcasted_iota(jnp.int32, (rank, rank), 1)
    sub = lax.broadcasted_iota(jnp.int32, (PANEL, rank), 0)
    lane = lax.broadcasted_iota(jnp.int32, (PANEL, rank), 1)

    def panel(p, carry):
        first = pl.multiple_of(p * PANEL, PANEL)
        done = eliminate(state_ref[pl.ds(first, PANEL), :], first)
        lower = jnp.where((lane > first + sub) & (lane < first + PANEL), 0.0, done)
        a, b, c = thirds(done)
        d, e, f = thirds(lower)
        step = dot(
            jnp.concatenate([a, a, b, b, a, c], axis=0), jnp.concatenate([d, e, d, e, f, d], axis=0), TN
        )
        old = state_ref[...]
        fresh = jnp.where((col >= first) & (col < first + PANEL), 0.0, old) - step
        state_ref[...] = jnp.where(row >= first + PANEL, fresh, old)
        state_ref[pl.ds(first, PANEL), :] = done
        return carry

    lax.fori_loop(begin, end, panel, 0)


def factor_left(count, place, own, other):
    rank = own.shape[1]
    chunk = rank // count

    def first(place_ref, own_ref, other_ref, state_ref):
        for j in range(count):
            part = (other_ref if j % 2 else own_ref)[j // 2 * chunk:(j // 2 + 1) * chunk, :]
            state_ref[pl.ds(pl.multiple_of((place_ref[0] ^ j) * chunk, chunk), chunk), :] = part
        factor_panels(state_ref, 0, rank // PANEL // 2)

    return call(first, "factor_first", struct(rank, rank), [place, own, other], flops=FACTOR, nbytes=131072)


def factor_rest(state):
    rank = state.shape[0]

    def rest(in_ref, out_ref):
        out_ref[...] = in_ref[...]
        factor_panels(out_ref, rank // PANEL // 2, rank // PANEL)
        out_ref[...] = lower_part(out_ref[...])

    return call(rest, "factor_rest", struct(rank, rank), [state], flops=FACTOR, nbytes=131072)


def factor_right(one, two):
    rank = one.shape[0]

    def first(one_ref, two_ref, gram_ref, state_ref):
        gram = one_ref[...] + two_ref[...]
        gram_ref[...] = gram
        state_ref[...] = gram
        factor_panels(state_ref, 0, rank // PANEL // 2)

    return call(first, "factor_first", [struct(rank, rank)] * 2, [one, two], flops=FACTOR, nbytes=131072)


def lower_part(x):
    row = lax.broadcasted_iota(jnp.int32, x.shape, 0)
    col = lax.broadcasted_iota(jnp.int32, x.shape, 1)
    return jnp.where(row >= col, x, 0.0)


def last_factor(one, two, right, scale):
    def body(one_ref, two_ref, right_ref, out_ref, state_ref):
        rank = state_ref.shape[0]
        state_ref[...] = one_ref[...] + two_ref[...]
        factor_panels(state_ref, 0, rank // PANEL)
        inv_high, inv_low = split(scale * lower_part(state_ref[...]))
        high, low = split(right_ref[...].T)
        both = jnp.concatenate([inv_high, inv_low], axis=0)
        wide = dot(high, both, NT)
        out_ref[...] = wide[:, :rank] + wide[:, rank:] + dot(low, inv_high, NT)

    rank, width = right.shape
    return call(body, "last_factor", struct(width, rank), [one, two, right], [pltpu.VMEM((rank, rank), F32)],
                flops=2 * FACTOR, nbytes=2_000_000)


def sum_halves(top, bottom, axis, beside=None):
    masks = masks_of(axis)
    for one, two in zip(masks[:-1], masks[:0:-1]):
        other_top, other_bottom = swap(top, axis, one), swap(bottom, axis, two)
        top, bottom = top + other_top, bottom + other_bottom
    if beside is not None:
        top, bottom, beside = lax.optimization_barrier((top, bottom, beside))
    return (top, swap(top, axis, masks[-1]), bottom, swap(bottom, axis, masks[0])), beside


class Share:
    def __init__(self, x, order, lane):
        self.x, self.order, self.lane = x, order, lane

    def halve(self, mask, extra=None):
        rows = self.x.shape[0] // len(self.order)
        pick = [[i for i, j in enumerate(self.order) if bool(j & mask) == bit] for bit in (False, True)]
        keep, send = [
            jnp.concatenate([self.x[i * rows:(i + 1) * rows] for i in at], axis=0) for at in pick
        ]
        order = [self.order[i] for i in pick[0]]
        if extra is None:
            return Share(keep + swap(send, "row", mask), order, self.lane), None
        size = send.shape[0]
        step = mask // 2 * rows
        turned = [extra[i ^ step:(i ^ step) + rows] for i in range(0, extra.shape[0], rows)]
        turned = jnp.concatenate(turned, axis=0)
        cuts = [turned[i:i + size] for i in range(0, turned.shape[0], size)]
        got = swap(jnp.concatenate([send, *cuts], axis=1), "row", mask)
        width, wide = send.shape[1], extra.shape[1]
        back = [got[:, width + i * wide:width + (i + 1) * wide] for i in range(len(cuts))]
        return Share(keep + got[:, :width], order, self.lane), extra + jnp.concatenate(back, axis=0)

    def fetch(self, mask):
        got = swap(self.x, "row", mask)
        return Share(got, [j ^ mask for j in self.order], self.lane)

    def join(self, other):
        return Share(jnp.concatenate([self.x, other.x], axis=0), self.order + other.order, self.lane)


def sum_rows(keep, send, count, rank):
    both = keep + swap(send, "row", 1)
    width = both.shape[1] - rank
    cut = width // rank // 2 * rank
    order = list(range(0, count, 2))
    one, two = Share(both[:, :cut], order, 0), Share(both[:, cut:width], order, cut)
    gram = both[:, width:]
    masks = masks_of("row")[1:]
    for up, down in zip(masks, reversed(masks)):
        one, gram = one.halve(up, gram)
        two, _ = two.halve(down)
    one.x, two.x, gram = lax.optimization_barrier((one.x, two.x, gram))
    return one, two, gram, swap(gram, "row", 1)


def gather_rows(one, two, beside):
    masks = masks_of("row")[1:]
    pieces = [one, two]
    state = beside[0]
    steps = list(beside[1:])
    for down, up in zip(reversed(masks), masks):
        more = [one.fetch(down), two.fetch(up)]
        if steps:
            state = steps.pop(0)(state)
        one, two = one.join(more[0]), two.join(more[1])
        one.x, two.x, state = lax.optimization_barrier((one.x, two.x, state))
        pieces += more
    pieces += [one.fetch(1), two.fetch(1)]
    return [(p.lane, p.order, p.x) for p in pieces], state


def shards(momentum, grad, basis):
    count = lax.axis_size("row")
    rank = basis.shape[1]
    width = momentum.shape[1]
    row_scale = float(momentum.shape[0] * count) ** 0.5
    col_scale = float(width * lax.axis_size("col")) ** 0.5
    place = lax.axis_index("row").astype(jnp.int32).reshape(1)
    high, low, top, bottom = start(momentum, grad, basis)
    halves, _ = sum_halves(top, bottom, "col")
    proj, keep, send = pull(count, place, halves, high, low)
    one, two, own, other = sum_rows(keep, send, count, rank)
    first = lambda grams: factor_left(count, place, *grams)
    pieces, inv = gather_rows(one, two, [(own, other), first, factor_rest])
    right_a, gram = normal(count, place, inv, pieces, width)
    left_a, top, bottom = push(inv, proj, high, low, right_a)
    masks = masks_of("col")
    for mask in masks[:-1]:
        gram = gram + swap(gram, "col", mask)
    top, bottom, gram = lax.optimization_barrier((top, bottom, gram))
    gram, state = factor_right(gram, swap(gram, "col", masks[-1]))
    halves, state = sum_halves(top, bottom, "col", state)
    inv = factor_rest(state)
    proj, keep, send = pull(count, place, halves, high, low, (left_a, right_a, gram, inv))
    one, two, own, other = sum_rows(keep, send, count, rank)
    pieces, inv = gather_rows(one, two, [(own, other), first, factor_rest])
    right_b, gram = normal(count, place, inv, pieces, width)
    gram = sum_part(gram, "col")
    momentum_out, lefts = finish(momentum, grad, left_a, proj, inv, right_a, right_b, row_scale)
    return momentum_out, lefts, last_factor(*gram, right_b, col_scale)


def solution(mesh):
    in_specs = (P("row", "col"), P("row", "col"), P("col", None))
    out_specs = (P("row", "col"), P(None, "row", None), P("col", None))
    return jax.shard_map(shards, mesh=mesh, in_specs=in_specs, out_specs=out_specs, check_vma=False)
```

```python
import jax
import jax.numpy as jnp
from jax import lax
from jax.experimental import pallas as pl
from jax.experimental.pallas import tpu as pltpu
from jax.sharding import PartitionSpec as P

F32 = jnp.float32
BF16 = jnp.bfloat16
HIGHEST = lax.Precision.HIGHEST
VMEM = pl.BlockSpec(memory_space=pltpu.VMEM)
SMEM = pl.BlockSpec(memory_space=pltpu.SMEM)
NN = (((1,), (0,)), ((), ()))
NT = (((1,), (1,)), ((), ()))
TN = (((0,), (0,)), ((), ()))
KEEP = 0.95
PANEL = 16
FACTOR = 1_500_000_000


def masks_of(axis):
    size = lax.axis_size(axis)
    masks = []
    mask = 1
    while mask < size:
        masks.append(mask)
        mask *= 2
    assert mask == size
    return masks


def swap(x, axis, even, odd):
    row_count, col_count = lax.axis_size("row"), lax.axis_size("col")
    pairs = []
    for row in range(row_count):
        mask = odd if row % 2 else even
        for col in range(col_count):
            to = (row ^ mask) * col_count + col if axis == "row" else row * col_count + (col ^ mask)
            pairs.append((row * col_count + col, to))
    return lax.ppermute(x, ("row", "col"), pairs)


def backward(slot, count):
    out, bit = 0, 1
    while bit < count:
        out = out * 2 + (slot // bit) % 2
        bit *= 2
    return out


def chunk_at(place, slot, count, other=False):
    if other:
        place = place ^ 1
    half = count // 2
    return place ^ jnp.where(place % 2 == 0, 2 * backward(slot, half), 2 * slot)


def split(x):
    high = x.astype(BF16)
    return high, (x - high.astype(F32)).astype(BF16)


def dot(a, b, dims=NN):
    return lax.dot_general(a, b, dims, preferred_element_type=F32)


def exact(a, b, dims=NN):
    return lax.dot_general(a, b, dims, precision=HIGHEST, preferred_element_type=F32)


def tiles(width, most=256):
    return [(start, min(most, width - start)) for start in range(0, width, most)]


def struct(*shape, dtype=F32):
    return jax.ShapeDtypeStruct(shape, dtype)


def call(body, name, out, ins, scratch=(), flops=0, nbytes=0, **kw):
    return pl.pallas_call(
        body,
        out_shape=out,
        in_specs=[SMEM if x.dtype == jnp.int32 else VMEM for x in ins],
        out_specs=jax.tree.map(lambda _: VMEM, out),
        scratch_shapes=list(scratch),
        name=name,
        compiler_params=pltpu.CompilerParams(vmem_limit_bytes=24 * 2**20),
        cost_estimate=pl.CostEstimate(flops=flops, bytes_accessed=nbytes, transcendentals=0),
        **kw,
    )(*ins)


def start(momentum, grad, basis):
    rows, cols = momentum.shape
    rank = basis.shape[1]
    steps = 4
    block = rows // steps

    def body(momentum_hbm, grad_hbm, basis_hbm, high_ref, low_ref, proj_ref, momentum_ref, grad_ref, basis_ref, both_ref, sems):
        whole = pltpu.make_async_copy(basis_hbm, basis_ref, sems.at[0])
        whole.start()
        copies = []
        for i in range(steps):
            at = pl.ds(i * block, block)
            pair = (
                pltpu.make_async_copy(momentum_hbm.at[at], momentum_ref.at[at], sems.at[1 + 2 * i]),
                pltpu.make_async_copy(grad_hbm.at[at], grad_ref.at[at], sems.at[2 + 2 * i]),
            )
            for copy in pair:
                copy.start()
            copies.append(pair)
        whole.wait()
        high, low = split(basis_ref[...])
        both_ref[:, :rank] = high
        both_ref[:, rank:] = low
        for i in range(steps):
            for copy in copies[i]:
                copy.wait()
            at = pl.ds(i * block, block)
            high, low = split(momentum_ref[at, :] + grad_ref[at, :].astype(F32))
            high_ref[at, :] = high
            low_ref[at, :] = low
            wide = dot(high, both_ref[...])
            proj_ref[at, :] = wide[:, :rank] + wide[:, rank:] + dot(low, both_ref[:, :rank])

    return pl.pallas_call(
        body,
        in_specs=[pl.BlockSpec(memory_space=pltpu.HBM)] * 3,
        out_specs=[VMEM] * 3,
        out_shape=[struct(rows, cols, dtype=BF16)] * 2 + [struct(rows, rank)],
        scratch_shapes=[
            pltpu.VMEM((rows, cols), F32),
            pltpu.VMEM((rows, cols), BF16),
            pltpu.VMEM((cols, rank), F32),
            pltpu.VMEM((cols, 2 * rank), BF16),
            pltpu.SemaphoreType.DMA((1 + 2 * steps,)),
        ],
        name="start",
        compiler_params=pltpu.CompilerParams(vmem_limit_bytes=24 * 2**20),
    )(*(pltpu.with_memory_space_constraint(x, pltpu.HBM) for x in (momentum, grad, basis)))


def pull_rows(turned, proj, high_ref, low_ref, cross, right_ref, out_ref):
    half = turned.shape[0]
    width = high_ref.shape[1]
    high, low = split(turned)
    both = jnp.concatenate([high, low], axis=0)
    for at, size in tiles(width):
        wide = dot(both, high_ref[:, at:at + size])
        out = wide[:half] + wide[half:] + dot(high, low_ref[:, at:at + size])
        if cross is not None:
            right_high, right_low = split(right_ref[:, at:at + size])
            wide = dot(jnp.concatenate(cross, axis=0), right_high)
            out = out + (wide[:half] + wide[half:] + dot(cross[0], right_low))
        out_ref[:, at:at + size] = out
    out_ref[:, width:] = exact(turned, proj)


def pull_send(count, place, one, two, high, low, before=None):
    rows, width = high.shape
    rank = one.shape[1]
    chunk = rank // count

    def body(place_ref, one_ref, two_ref, high_ref, low_ref, *rest):
        proj = one_ref[...] + two_ref[...]
        left_ref = right_ref = None
        if before is not None:
            left_ref, right_ref, gram_ref, inv_ref = rest[:4]
            proj = proj - KEEP * exact(left_ref[...], gram_ref[...])
            proj = exact(proj, inv_ref[...], NT)
        proj_ref, keep_ref, send_ref, turned_ref = rest[-4:]
        proj_ref[...] = proj
        turned_ref[...] = proj.T

        def pick(other):
            at = [chunk_at(place_ref[0], t, count, other) * chunk for t in range(count // 2)]
            return jnp.concatenate([turned_ref[pl.ds(pl.multiple_of(x, chunk), chunk), :] for x in at], axis=0)

        keep_ref[...] = pick(False)
        turned = pick(True)
        cross = None if before is None else split(-KEEP * exact(turned, left_ref[...]))
        pull_rows(turned, proj, high_ref, low_ref, cross, right_ref, send_ref)

    out = [struct(rows, rank), struct(rank // 2, rows), struct(rank // 2, width + rank)]
    ins = [place, one, two, high, low] + list(before or [])
    return call(body, "pull_send", out, ins, [pltpu.VMEM((rank, rows), F32)], flops=500_000_000, nbytes=5_000_000)


def pull_keep(turned, proj, high, low, before=None):
    rows, width = high.shape
    rank = proj.shape[1]

    def body(turned_ref, proj_ref, high_ref, low_ref, *rest):
        turned = turned_ref[...]
        cross = right_ref = None
        if before is not None:
            left_ref, right_ref = rest[:2]
            cross = split(-KEEP * exact(turned, left_ref[...]))
        pull_rows(turned, proj_ref[...], high_ref, low_ref, cross, right_ref, rest[-1])

    ins = [turned, proj, high, low] + list(before or [])[:2]
    return call(body, "pull_keep", struct(rank // 2, width + rank), ins, flops=500_000_000, nbytes=5_000_000)


def normal(count, place, inv, own, other):
    rank = inv.shape[0]
    width = other.shape[1]
    chunk = rank // count

    def body(place_ref, inv_ref, other_ref, *rest):
        right_ref, gram_ref, raw_ref = rest[len(own):]
        place = place_ref[0]

        def put(piece, first, is_other):
            for i in range(piece.shape[0] // chunk):
                at = chunk_at(place, first + i, count, is_other) * chunk
                raw_ref[pl.ds(pl.multiple_of(at, chunk), chunk), :] = piece[i * chunk:(i + 1) * chunk, :]
            return first + piece.shape[0] // chunk

        slot = 0
        for piece in rest[:len(own)]:
            slot = put(piece, slot, False)
        put(other_ref, 0, True)
        inv_high, inv_low = split(inv_ref[...])
        inv_both = jnp.concatenate([inv_high, inv_low], axis=0)
        gram = jnp.zeros((rank, rank), F32)
        for at, size in tiles(width):
            raw_high, raw_low = split(raw_ref[:, at:at + size])
            wide = dot(inv_both, raw_high)
            right = wide[:rank] + wide[rank:] + dot(inv_high, raw_low)
            right_ref[:, at:at + size] = right
            high, low = split(right)
            wide = dot(jnp.concatenate([high, low], axis=0), high, NT)
            gram = gram + (wide[:rank] + wide[rank:] + dot(high, low, NT))
        gram_ref[...] = gram

    return call(body, "normal", [struct(rank, width), struct(rank, rank)], [place, inv, other, *own],
                [pltpu.VMEM((rank, width), F32)], flops=500_000_000, nbytes=2_000_000)


def push(high, low, right):
    rows, width = high.shape
    rank = right.shape[0]

    def body(high_ref, low_ref, right_ref, out_ref):
        image = None
        for at, size in tiles(width):
            right_high, right_low = split(right_ref[:, at:at + size])
            wide = dot(high_ref[:, at:at + size], jnp.concatenate([right_high, right_low], axis=0), NT)
            part = wide[:, :rank] + wide[:, rank:] + dot(low_ref[:, at:at + size], right_high, NT)
            image = part if image is None else image + part
        out_ref[...] = image

    return call(body, "push", struct(rows, rank), [high, low, right], flops=700_000_000, nbytes=5_000_000)


def left_of(proj, inv):
    def body(proj_ref, inv_ref, out_ref):
        out_ref[...] = exact(proj_ref[...], inv_ref[...], NT)

    return call(body, "left", struct(*proj.shape), [proj, inv], flops=100_000_000, nbytes=600_000)


def deflate(base, left, right, name, last=None):
    rows, cols = base[0].shape
    rank = left.shape[1]
    block = rows // 4
    tile = pl.BlockSpec((block, cols), lambda i: (i, 0))
    left_tile = pl.BlockSpec((block, rank), lambda i: (i, 0))
    right_tile = pl.BlockSpec((rank, cols), lambda i: (0, 0))

    def body(*refs):
        base_refs = refs[:len(base)]
        left_ref, right_ref = refs[len(base):len(base) + 2]
        high_ref, low_ref = refs[-2:]
        out_ref = refs[-3] if last is None else refs[-4]

        @pl.when(pl.program_id(0) == 0)
        def _():
            high, low = split(KEEP * right_ref[...])
            high_ref[...] = high
            low_ref[...] = low

        left = left_ref[...]
        if last is not None:
            refs[-3][0] = last[1] * refs[len(base) + 2][...]
            refs[-3][1] = last[1] * left
        high, low = split(left)
        for at, size in tiles(cols):
            right_high = high_ref[:, at:at + size]
            wide = dot(jnp.concatenate([high, low], axis=0), right_high)
            outer = wide[:block] + wide[block:] + dot(high, low_ref[:, at:at + size])
            total = base_refs[0][:, at:at + size]
            for ref in base_refs[1:]:
                total = total + ref[:, at:at + size].astype(F32)
            out_ref[:, at:at + size] = total - outer

    ins, in_specs = [*base, left, right], [tile] * len(base) + [left_tile, right_tile]
    out, out_specs = [struct(rows, cols)], [tile]
    if last is not None:
        ins.append(last[0])
        in_specs.append(left_tile)
        out.append(struct(2, rows, rank))
        out_specs.append(pl.BlockSpec((2, block, rank), lambda i: (0, i, 0)))
    return pl.pallas_call(
        body,
        grid=(4,),
        in_specs=in_specs,
        out_specs=out_specs,
        out_shape=out,
        scratch_shapes=[pltpu.VMEM((rank, cols), BF16)] * 2,
        name=name,
        compiler_params=pltpu.CompilerParams(vmem_limit_bytes=24 * 2**20),
        cost_estimate=pl.CostEstimate(flops=1_500_000_000, bytes_accessed=12_000_000, transcendentals=0),
    )(*ins)


def eliminate(full, first):
    rank = full.shape[1]
    groups = PANEL // 8
    sub = lax.broadcasted_iota(jnp.int32, (8, rank), 0)
    lane = lax.broadcasted_iota(jnp.int32, (8, rank), 1)
    rolled = pltpu.roll(full, lax.rem(rank - first, rank), 1)
    rows = [full[8 * g:8 * g + 8] for g in range(groups)]
    cols = [
        [jnp.broadcast_to(rolled[8 * g:8 * g + 8, j:j + 1], (8, rank)) for g in range(groups)] for j in range(PANEL)
    ]

    def spread(x, j):
        return jnp.broadcast_to(x[j // 8][j % 8:j % 8 + 1], (8, rank))

    pivot = spread(cols[0], 0)
    for j in range(PANEL):
        at = j // 8
        root = lax.rsqrt(pivot)
        if j + 1 < PANEL:
            above = spread(cols[j + 1], j) * root
            pivot = spread(cols[j + 1], j + 1) - above * above
        below = sub > j % 8
        here = lane == first + j
        row = jnp.where(here, 1.0, spread(rows, j)) * root
        for g in range(at, groups):
            mult = cols[j][g] * root
            rest = jnp.where(here, 0.0, rows[g])
            if g == at:
                mult = jnp.where(below, mult, 0.0)
                rest = jnp.where(below, rest, rows[g])
            rest = rest - mult * row
            rows[g] = jnp.where(sub == j % 8, row, rest) if g == at else rest
            cols[j][g] = mult
        for k in range(j + 1, PANEL):
            across = spread(cols[k], j) * root
            for g in range(at, groups):
                cols[k][g] = cols[k][g] - cols[j][g] * across
    return jnp.concatenate(rows, axis=0)


def thirds(x):
    high = x.astype(BF16)
    rest = x - high.astype(F32)
    middle = rest.astype(BF16)
    return high, middle, (rest - middle.astype(F32)).astype(BF16)


def factor_panels(state_ref, begin, end):
    rank = state_ref.shape[0]
    row = lax.broadcasted_iota(jnp.int32, (rank, rank), 0)
    col = lax.broadcasted_iota(jnp.int32, (rank, rank), 1)
    sub = lax.broadcasted_iota(jnp.int32, (PANEL, rank), 0)
    lane = lax.broadcasted_iota(jnp.int32, (PANEL, rank), 1)

    def panel(p, carry):
        first = pl.multiple_of(p * PANEL, PANEL)
        done = eliminate(state_ref[pl.ds(first, PANEL), :], first)
        lower = jnp.where((lane > first + sub) & (lane < first + PANEL), 0.0, done)
        a, b, c = thirds(done)
        d, e, f = thirds(lower)
        step = dot(
            jnp.concatenate([a, a, b, b, a, c], axis=0), jnp.concatenate([d, e, d, e, f, d], axis=0), TN
        )
        old = state_ref[...]
        fresh = jnp.where((col >= first) & (col < first + PANEL), 0.0, old) - step
        state_ref[...] = jnp.where(row >= first + PANEL, fresh, old)
        state_ref[pl.ds(first, PANEL), :] = done
        return carry

    lax.fori_loop(begin, end, panel, 0)


def factor_left(count, place, own, other):
    rank = own.shape[1]
    chunk = rank // count

    def first(place_ref, own_ref, other_ref, state_ref):
        for ref, is_other in ((own_ref, False), (other_ref, True)):
            for t in range(count // 2):
                at = chunk_at(place_ref[0], t, count, is_other) * chunk
                state_ref[pl.ds(pl.multiple_of(at, chunk), chunk), :] = ref[t * chunk:(t + 1) * chunk, :]
        factor_panels(state_ref, 0, rank // PANEL // 2)

    return call(first, "factor_first", struct(rank, rank), [place, own, other], flops=FACTOR, nbytes=131072)


def factor_rest(state):
    rank = state.shape[0]

    def rest(in_ref, out_ref):
        out_ref[...] = in_ref[...]
        factor_panels(out_ref, rank // PANEL // 2, rank // PANEL)
        out_ref[...] = lower_part(out_ref[...])

    return call(rest, "factor_rest", struct(rank, rank), [state], flops=FACTOR, nbytes=131072)


def factor_right(one, two):
    rank = one.shape[0]

    def first(one_ref, two_ref, gram_ref, state_ref):
        gram = one_ref[...] + two_ref[...]
        gram_ref[...] = gram
        state_ref[...] = gram
        factor_panels(state_ref, 0, rank // PANEL // 2)

    return call(first, "factor_first", [struct(rank, rank)] * 2, [one, two], flops=FACTOR, nbytes=131072)


def lower_part(x):
    row = lax.broadcasted_iota(jnp.int32, x.shape, 0)
    col = lax.broadcasted_iota(jnp.int32, x.shape, 1)
    return jnp.where(row >= col, x, 0.0)


def turn(right):
    rank, width = right.shape

    def body(right_ref, high_ref, low_ref):
        high, low = split(right_ref[...].T)
        high_ref[...] = high
        low_ref[...] = low

    return call(body, "turn", [struct(width, rank, dtype=BF16)] * 2, [right], flops=100_000_000, nbytes=2_000_000)


def last_factor(one, two, high, low, scale):
    def body(one_ref, two_ref, high_ref, low_ref, out_ref, state_ref):
        rank = state_ref.shape[0]
        state_ref[...] = one_ref[...] + two_ref[...]
        factor_panels(state_ref, 0, rank // PANEL)
        inv_high, inv_low = split(scale * lower_part(state_ref[...]))
        both = jnp.concatenate([inv_high, inv_low], axis=0)
        wide = dot(high_ref[...], both, NT)
        out_ref[...] = wide[:, :rank] + wide[:, rank:] + dot(low_ref[...], inv_high, NT)

    width, rank = high.shape
    return call(body, "last_factor", struct(width, rank), [one, two, high, low], [pltpu.VMEM((rank, rank), F32)],
                flops=2 * FACTOR, nbytes=2_000_000)


def sum_cols(x):
    masks = masks_of("col")
    for even, odd in zip(masks[:-1], masks[:0:-1]):
        x = x + swap(x, "col", even, odd)
    return x, lambda y: swap(y, "col", masks[-1], masks[0])


def sum_rows(keep, send, count, rank, beside=None):
    x = keep + swap(send, "row", 1, 1)
    width = x.shape[1] - rank
    gram = x[:, width:]
    x = x[:, :width]
    chunk = rank // count
    slots = count // 2
    masks = masks_of("row")[1:]
    bit = slots // 2
    for even, odd in zip(masks, reversed(masks)):
        size = bit * chunk
        cuts = [gram[(t ^ bit) * chunk:((t ^ bit) + 1) * chunk] for t in range(slots)]
        cuts = [jnp.concatenate(cuts[i:i + bit], axis=0) for i in range(0, slots, bit)]
        got = swap(jnp.concatenate([x[size:], *cuts], axis=1), "row", even, odd)
        back = [got[:, width + i * rank:width + (i + 1) * rank] for i in range(slots // bit)]
        x = x[:size] + got[:, :width]
        gram = gram + jnp.concatenate(back, axis=0)
        if beside is not None:
            x, gram, beside = lax.optimization_barrier((x, gram, beside))
        bit //= 2
    x, gram = lax.optimization_barrier((x, gram))
    return x, gram, swap(gram, "row", 1, 1), beside


def gather_rows(x, state, steps):
    masks = masks_of("row")[1:]
    own = [x]
    steps = list(steps)
    for even, odd in zip(reversed(masks), masks):
        more = swap(x, "row", even, odd)
        if steps:
            state = steps.pop(0)(state)
        x = jnp.concatenate([x, more], axis=0)
        x, state = lax.optimization_barrier((x, state))
        own.append(more)
    return own, swap(x, "row", 1, 1), state


def shards(momentum, grad, basis):
    count = lax.axis_size("row")
    rank = basis.shape[1]
    width = momentum.shape[1]
    row_scale = float(momentum.shape[0] * count) ** 0.5
    col_scale = float(width * lax.axis_size("col")) ** 0.5
    place = lax.axis_index("row").astype(jnp.int32).reshape(1)

    def left_side(one, two, before, beside):
        proj, turned, send = pull_send(count, place, one, two, high, low, before)
        keep = pull_keep(turned, proj, high, low, before)
        raw, own, other, beside = sum_rows(keep, send, count, rank, beside)

        def first(grams):
            return factor_left(count, place, *grams)

        def rest(state):
            inv = factor_rest(state)
            return inv, left_of(proj, inv)

        own, other, (inv, left) = gather_rows(raw, (own, other), (first, rest))
        return left, *normal(count, place, inv, own, other), beside

    high, low, proj = start(momentum, grad, basis)
    one, last_swap = sum_cols(proj)
    left_a, right_a, gram, _ = left_side(one, last_swap(one), None, None)

    image = push(high, low, right_a)
    gram, last_swap = sum_cols(gram)
    image, gram = lax.optimization_barrier((image, gram))
    gram, state = factor_right(gram, last_swap(gram))
    one, last_swap = sum_cols(image)
    one, state = lax.optimization_barrier((one, state))
    two = last_swap(one)
    inv = factor_rest(state)

    base = deflate([momentum, grad], left_a, right_a, "deflate")
    left_b, right_b, gram, base = left_side(one, two, (left_a, right_a, gram, inv), base)

    gram, last_swap = sum_cols(gram)
    momentum_out, lefts = deflate(base, left_b, right_b, "finish", (left_a, row_scale))
    gram, momentum_out = lax.optimization_barrier((gram, momentum_out))
    turned = turn(right_b)
    return momentum_out, lefts, last_factor(gram, last_swap(gram), *turned, col_scale)


def solution(mesh):
    in_specs = (P("row", "col"), P("row", "col"), P("col", None))
    out_specs = (P("row", "col"), P(None, "row", None), P("col", None))
    return jax.shard_map(shards, mesh=mesh, in_specs=in_specs, out_specs=out_specs, check_vma=False)
```

```python
import jax
import jax.numpy as jnp
from jax import lax
from jax.experimental import pallas as pl
from jax.experimental.pallas import tpu as pltpu
from jax.sharding import PartitionSpec as P

F32 = jnp.float32
BF16 = jnp.bfloat16
HIGHEST = lax.Precision.HIGHEST
VMEM = pl.BlockSpec(memory_space=pltpu.VMEM)
SMEM = pl.BlockSpec(memory_space=pltpu.SMEM)
NN = (((1,), (0,)), ((), ()))
NT = (((1,), (1,)), ((), ()))
TN = (((0,), (0,)), ((), ()))
KEEP = 0.95
PANEL = 16
FACTOR = 1_500_000_000


def masks_of(axis):
    size = lax.axis_size(axis)
    masks = []
    mask = 1
    while mask < size:
        masks.append(mask)
        mask *= 2
    assert mask == size
    return masks


def swap(x, axis, even, odd):
    row_count, col_count = lax.axis_size("row"), lax.axis_size("col")
    pairs = []
    for row in range(row_count):
        mask = odd if row % 2 else even
        for col in range(col_count):
            to = (row ^ mask) * col_count + col if axis == "row" else row * col_count + (col ^ mask)
            pairs.append((row * col_count + col, to))
    return lax.ppermute(x, ("row", "col"), pairs)


def chunk_at(place, slot, other=False):
    return place ^ (2 * slot + (1 if other else 0))


def split(x):
    high = x.astype(BF16)
    return high, (x - high.astype(F32)).astype(BF16)


def dot(a, b, dims=NN):
    return lax.dot_general(a, b, dims, preferred_element_type=F32)


def exact(a, b, dims=NN):
    return lax.dot_general(a, b, dims, precision=HIGHEST, preferred_element_type=F32)


def tiles(width, most=256):
    return [(start, min(most, width - start)) for start in range(0, width, most)]


def struct(*shape, dtype=F32):
    return jax.ShapeDtypeStruct(shape, dtype)


def call(body, name, out, ins, scratch=(), flops=0, nbytes=0, **kw):
    return pl.pallas_call(
        body,
        out_shape=out,
        in_specs=[SMEM if x.dtype == jnp.int32 else VMEM for x in ins],
        out_specs=jax.tree.map(lambda _: VMEM, out),
        scratch_shapes=list(scratch),
        name=name,
        compiler_params=pltpu.CompilerParams(vmem_limit_bytes=24 * 2**20),
        cost_estimate=pl.CostEstimate(flops=flops, bytes_accessed=nbytes, transcendentals=0),
        **kw,
    )(*ins)


def start(momentum, grad, basis):
    rows, cols = momentum.shape
    rank = basis.shape[1]
    steps = 4
    block = rows // steps

    def body(momentum_hbm, grad_hbm, basis_hbm, high_ref, low_ref, proj_ref, momentum_ref, grad_ref, basis_ref, both_ref, sems):
        whole = pltpu.make_async_copy(basis_hbm, basis_ref, sems.at[0])
        whole.start()
        copies = []
        for i in range(steps):
            at = pl.ds(i * block, block)
            pair = (
                pltpu.make_async_copy(momentum_hbm.at[at], momentum_ref.at[at], sems.at[1 + 2 * i]),
                pltpu.make_async_copy(grad_hbm.at[at], grad_ref.at[at], sems.at[2 + 2 * i]),
            )
            for copy in pair:
                copy.start()
            copies.append(pair)
        whole.wait()
        high, low = split(basis_ref[...])
        both_ref[:, :rank] = high
        both_ref[:, rank:] = low
        for i in range(steps):
            for copy in copies[i]:
                copy.wait()
            at = pl.ds(i * block, block)
            high, low = split(momentum_ref[at, :] + grad_ref[at, :].astype(F32))
            high_ref[at, :] = high
            low_ref[at, :] = low
            wide = dot(high, both_ref[...])
            proj_ref[at, :] = wide[:, :rank] + wide[:, rank:] + dot(low, both_ref[:, :rank])

    return pl.pallas_call(
        body,
        in_specs=[pl.BlockSpec(memory_space=pltpu.HBM)] * 3,
        out_specs=[VMEM] * 3,
        out_shape=[struct(rows, cols, dtype=BF16)] * 2 + [struct(rows, rank)],
        scratch_shapes=[
            pltpu.VMEM((rows, cols), F32),
            pltpu.VMEM((rows, cols), BF16),
            pltpu.VMEM((cols, rank), F32),
            pltpu.VMEM((cols, 2 * rank), BF16),
            pltpu.SemaphoreType.DMA((1 + 2 * steps,)),
        ],
        name="start",
        compiler_params=pltpu.CompilerParams(vmem_limit_bytes=24 * 2**20),
    )(*(pltpu.with_memory_space_constraint(x, pltpu.HBM) for x in (momentum, grad, basis)))


def pull_rows(turned, proj, high_ref, low_ref, cross, right_ref, out_ref):
    half = turned.shape[0]
    width = high_ref.shape[1]
    high, low = split(turned)
    both = jnp.concatenate([high, low], axis=0)
    for at, size in tiles(width):
        wide = dot(both, high_ref[:, at:at + size])
        out = wide[:half] + wide[half:] + dot(high, low_ref[:, at:at + size])
        if cross is not None:
            right_high, right_low = split(right_ref[:, at:at + size])
            wide = dot(jnp.concatenate(cross, axis=0), right_high)
            out = out + (wide[:half] + wide[half:] + dot(cross[0], right_low))
        out_ref[:, at:at + size] = out
    return gram_rows(high, low, both, proj)


def gram_rows(high, low, both, proj):
    half, rank = high.shape[0], proj.shape[1]
    proj_high, proj_low = split(proj)
    wide = dot(both, jnp.concatenate([proj_high, proj_low], axis=1))
    return wide[:half, :rank] + wide[:half, rank:] + wide[half:, :rank]


def put_gram(place, gram, out_ref, width, chunk):
    for t in range(gram.shape[0] // chunk):
        at = pl.multiple_of((place // 2 ^ t) * chunk, chunk)
        out_ref[pl.ds(at, chunk), width:] = gram[t * chunk:(t + 1) * chunk]


def pull_send(count, place, one, two, high, low, before=None):
    rows, width = high.shape
    rank = before[0].shape[1] if before is not None else one.shape[1]
    chunk = rank // count

    def body(place_ref, one_ref, two_ref, high_ref, low_ref, *rest):
        place = place_ref[0]
        proj = one_ref[:rows, :] + two_ref[...]
        left_ref = right_ref = None
        if before is not None:
            left_ref, right_ref, gram_ref, inv_ref = rest[:4]
            proj = proj - KEEP * exact(left_ref[...], gram_ref[...])
            proj = exact(proj, inv_ref[...], NT)
        proj_ref, keep_ref, send_ref, turned_ref = rest[-4:]
        proj_ref[...] = proj
        turned_ref[...] = proj.T

        def pick(other):
            at = [chunk_at(place, t, other) * chunk for t in range(count // 2)]
            return jnp.concatenate([turned_ref[pl.ds(pl.multiple_of(x, chunk), chunk), :] for x in at], axis=0)

        keep_ref[...] = pick(False)
        turned = pick(True)
        cross = None if before is None else split(-KEEP * exact(turned, left_ref[...]))
        gram = pull_rows(turned, proj, high_ref, low_ref, cross, right_ref, send_ref)
        put_gram(place, gram, send_ref, width, chunk)

    out = [struct(rows, rank), struct(rank // 2, rows), struct(rank // 2, width + rank)]
    ins = [place, one, two, high, low] + list(before or [])
    return call(body, "pull_send", out, ins, [pltpu.VMEM((rank, rows), F32)], flops=500_000_000, nbytes=5_000_000)


def pull_keep(count, place, turned, proj, high, low, before=None):
    rows, width = high.shape
    rank = proj.shape[1]
    chunk = rank // count

    def body(place_ref, turned_ref, proj_ref, high_ref, low_ref, *rest):
        place = place_ref[0]
        turned = turned_ref[...]
        cross = right_ref = None
        if before is not None:
            left_ref, right_ref = rest[:2]
            cross = split(-KEEP * exact(turned, left_ref[...]))
        gram = pull_rows(turned, proj_ref[...], high_ref, low_ref, cross, right_ref, rest[-1])
        put_gram(place, gram, rest[-1], width, chunk)

    ins = [place, turned, proj, high, low] + list(before or [])[:2]
    return call(body, "pull_keep", struct(rank // 2, width + rank), ins, flops=500_000_000, nbytes=5_000_000)


def normal(count, place, inv, own, other, high=None, low=None):
    rank = inv.shape[0]
    width = own[0].shape[1]
    chunk = rank // count
    push = high is not None
    rows = high.shape[0] if push else 0

    def body(place_ref, inv_ref, *rest):
        pieces, rest = rest[:count], rest[count:]
        if push:
            work_high, work_low, right_ref, out_ref, raw_ref = rest
        else:
            right_ref, out_ref, raw_ref = rest
        place = place_ref[0]
        for i, piece in enumerate(pieces):
            at = chunk_at(place, i % (count // 2), i >= count // 2) * chunk
            raw_ref[pl.ds(pl.multiple_of(at, chunk), chunk), :] = piece[...]
        inv_high, inv_low = split(inv_ref[...])
        inv_both = jnp.concatenate([inv_high, inv_low], axis=0)
        gram = jnp.zeros((rank, rank), F32)
        image = jnp.zeros((rows, rank), F32) if push else None
        for at, size in tiles(width):
            raw_high, raw_low = split(raw_ref[:, at:at + size])
            wide = dot(inv_both, raw_high)
            right = wide[:rank] + wide[rank:] + dot(inv_high, raw_low)
            right_ref[:, at:at + size] = right
            high, low = split(right)
            both = jnp.concatenate([high, low], axis=0)
            wide = dot(both, high, NT)
            gram = gram + (wide[:rank] + wide[rank:] + dot(high, low, NT))
            if push:
                wide = dot(work_high[:, at:at + size], both, NT)
                image = image + (wide[:, :rank] + wide[:, rank:] + dot(work_low[:, at:at + size], high, NT))
        if push:
            out_ref[:rows, :] = image
        out_ref[rows:, :] = gram

    ins = [place, inv, *own, *other] + ([high, low] if push else [])
    return call(body, "normal", [struct(rank, width), struct(rows + rank, rank)], ins,
                [pltpu.VMEM((rank, width), F32)], flops=1_000_000_000, nbytes=5_000_000)


def left_of(proj, inv):
    def body(proj_ref, inv_ref, out_ref):
        out_ref[...] = exact(proj_ref[...], inv_ref[...], NT)

    return call(body, "left", struct(*proj.shape), [proj, inv], flops=100_000_000, nbytes=600_000)


def outer_tile(left, right_high, right_low):
    high, low = split(left)
    rows = left.shape[0]
    wide = dot(jnp.concatenate([high, low], axis=0), right_high)
    return wide[:rows] + wide[rows:] + dot(high, right_low)


def deflate(momentum, grad, left, right):
    rows, cols = momentum.shape
    block = rows // 4

    def body(momentum_ref, grad_ref, left_ref, right_ref, out_ref):
        for at, size in tiles(cols):
            lanes = slice(at, at + size)
            right_high, right_low = split(KEEP * right_ref[:, lanes])
            for i in range(4):
                row = slice(i * block, (i + 1) * block)
                work = momentum_ref[row, lanes] + grad_ref[row, lanes].astype(F32)
                out_ref[row, lanes] = work - outer_tile(left_ref[row, :], right_high, right_low)

    return call(body, "deflate", struct(rows, cols), [momentum, grad, left, right], flops=1_500_000_000, nbytes=9_000_000)


def finish(base, left, right, before=None, scale=None, part=0):
    rows, cols = base.shape
    rank = left.shape[1]
    half = rows // 2
    block = half // 2
    first = part * half

    def body(base_ref, left_ref, right_ref, *rest):
        if part == 0:
            other_ref, out_ref, lefts_ref, stage_ref, high_ref, low_ref, sems = rest
            lefts_ref[0] = scale * other_ref[...]
            lefts_ref[1] = scale * left_ref[...]
        else:
            _, out_ref, stage_ref, high_ref, low_ref, sems = rest
        for at, size in tiles(cols):
            lanes = slice(at, at + size)
            high_ref[:, lanes], low_ref[:, lanes] = split(KEEP * right_ref[:, lanes])
        copies = []
        for i in range(2):
            row = slice(first + i * block, first + (i + 1) * block)
            for at, size in tiles(cols):
                lanes = slice(at, at + size)
                outer = outer_tile(left_ref[row, :], high_ref[:, lanes], low_ref[:, lanes])
                stage_ref[i, :, lanes] = base_ref[row, lanes] - outer
            copy = pltpu.make_async_copy(stage_ref.at[i], out_ref.at[pl.ds(first + i * block, block)], sems.at[i])
            copy.start()
            copies.append(copy)
        for copy in copies:
            copy.wait()

    hbm = pl.BlockSpec(memory_space=pltpu.HBM)
    out, out_specs = [struct(rows, cols)], [hbm]
    if part == 0:
        ins, in_specs, alias = [base, left, right, before], [VMEM] * 4, {}
        out.append(struct(2, rows, rank))
        out_specs.append(VMEM)
    else:
        ins, in_specs, alias = [base, left, right, before], [VMEM] * 3 + [hbm], {3: 0}
    return pl.pallas_call(
        body,
        in_specs=in_specs,
        out_specs=out_specs,
        out_shape=out,
        scratch_shapes=[pltpu.VMEM((2, block, cols), F32)] + [pltpu.VMEM((rank, cols), BF16)] * 2
        + [pltpu.SemaphoreType.DMA((2,))],
        input_output_aliases=alias,
        name="finish",
        compiler_params=pltpu.CompilerParams(vmem_limit_bytes=24 * 2**20),
        cost_estimate=pl.CostEstimate(flops=800_000_000, bytes_accessed=6_000_000, transcendentals=0),
    )(*ins)


def eliminate(full, first):
    rank = full.shape[1]
    groups = PANEL // 8
    sub = lax.broadcasted_iota(jnp.int32, (8, rank), 0)
    lane = lax.broadcasted_iota(jnp.int32, (8, rank), 1)
    rolled = pltpu.roll(full, lax.rem(rank - first, rank), 1)
    rows = [full[8 * g:8 * g + 8] for g in range(groups)]
    cols = [
        [jnp.broadcast_to(rolled[8 * g:8 * g + 8, j:j + 1], (8, rank)) for g in range(groups)] for j in range(PANEL)
    ]

    def spread(x, j):
        return jnp.broadcast_to(x[j // 8][j % 8:j % 8 + 1], (8, rank))

    pivot = spread(cols[0], 0)
    for j in range(PANEL):
        at = j // 8
        root = lax.rsqrt(pivot)
        if j + 1 < PANEL:
            above = spread(cols[j + 1], j) * root
            pivot = spread(cols[j + 1], j + 1) - above * above
        below = sub > j % 8
        here = lane == first + j
        row = jnp.where(here, 1.0, spread(rows, j)) * root
        for g in range(at, groups):
            mult = cols[j][g] * root
            rest = jnp.where(here, 0.0, rows[g])
            if g == at:
                mult = jnp.where(below, mult, 0.0)
                rest = jnp.where(below, rest, rows[g])
            rest = rest - mult * row
            rows[g] = jnp.where(sub == j % 8, row, rest) if g == at else rest
            cols[j][g] = mult
        for k in range(j + 1, PANEL):
            across = spread(cols[k], j) * root
            for g in range(at, groups):
                cols[k][g] = cols[k][g] - cols[j][g] * across
    return jnp.concatenate(rows, axis=0)


def thirds(x):
    high = x.astype(BF16)
    rest = x - high.astype(F32)
    middle = rest.astype(BF16)
    return high, middle, (rest - middle.astype(F32)).astype(BF16)


def factor_panels(state_ref):
    rank = state_ref.shape[0]
    row = lax.broadcasted_iota(jnp.int32, (rank, rank), 0)
    col = lax.broadcasted_iota(jnp.int32, (rank, rank), 1)
    sub = lax.broadcasted_iota(jnp.int32, (PANEL, rank), 0)
    lane = lax.broadcasted_iota(jnp.int32, (PANEL, rank), 1)

    def panel(p, carry):
        first = pl.multiple_of(p * PANEL, PANEL)
        done = eliminate(state_ref[pl.ds(first, PANEL), :], first)
        lower = jnp.where((lane > first + sub) & (lane < first + PANEL), 0.0, done)
        a, b, c = thirds(done)
        d, e, f = thirds(lower)
        step = dot(
            jnp.concatenate([a, a, b, b, a, c], axis=0), jnp.concatenate([d, e, d, e, f, d], axis=0), TN
        )
        old = state_ref[...]
        fresh = jnp.where((col >= first) & (col < first + PANEL), 0.0, old) - step
        state_ref[...] = jnp.where(row >= first + PANEL, fresh, old)
        state_ref[pl.ds(first, PANEL), :] = done
        return carry

    lax.fori_loop(0, rank // PANEL, panel, 0)


def factor_left(count, place, own, other):
    chunk, rank = own.shape[0], 2 * own.shape[1] // count

    def body(place_ref, own_ref, other_ref, out_ref):
        core = place_ref[0] % 2
        for t in range(count // 2):
            for ref, at in ((own_ref, 2 * t + core), (other_ref, 2 * t + 1 - core)):
                out_ref[pl.ds(pl.multiple_of(at * chunk, chunk), chunk), :] = ref[:, t * rank:(t + 1) * rank]
        factor_panels(out_ref)
        out_ref[...] = lower_part(out_ref[...])

    return call(body, "factor", struct(rank, rank), [place, own, other], flops=2 * FACTOR, nbytes=131072)


def factor_right(one, two, first):
    rank = one.shape[1]

    def body(one_ref, two_ref, gram_ref, out_ref):
        gram = one_ref[first:, :] + two_ref[...]
        gram_ref[...] = gram
        out_ref[...] = gram
        factor_panels(out_ref)
        out_ref[...] = lower_part(out_ref[...])

    return call(body, "factor", [struct(rank, rank)] * 2, [one, two], flops=2 * FACTOR, nbytes=131072)


def lower_part(x):
    row = lax.broadcasted_iota(jnp.int32, x.shape, 0)
    col = lax.broadcasted_iota(jnp.int32, x.shape, 1)
    return jnp.where(row >= col, x, 0.0)


def turn(right):
    rank, width = right.shape

    def body(right_ref, high_ref, low_ref):
        high, low = split(right_ref[...].T)
        high_ref[...] = high
        low_ref[...] = low

    return call(body, "turn", [struct(width, rank, dtype=BF16)] * 2, [right], flops=100_000_000, nbytes=2_000_000)


def last_factor(one, two, high, low, scale):
    def body(one_ref, two_ref, high_ref, low_ref, out_ref, state_ref):
        rank = state_ref.shape[0]
        state_ref[...] = one_ref[...] + two_ref[...]
        factor_panels(state_ref)
        inv_high, inv_low = split(scale * lower_part(state_ref[...]))
        both = jnp.concatenate([inv_high, inv_low], axis=0)
        wide = dot(high_ref[...], both, NT)
        out_ref[...] = wide[:, :rank] + wide[:, rank:] + dot(low_ref[...], inv_high, NT)

    width, rank = high.shape
    return call(body, "last_factor", struct(width, rank), [one, two, high, low], [pltpu.VMEM((rank, rank), F32)],
                flops=2 * FACTOR, nbytes=2_000_000)


def sum_cols(x):
    masks = masks_of("col")
    for even, odd in zip(masks[:-1], masks[:0:-1]):
        x = x + swap(x, "col", even, odd)
    return x, lambda y: swap(y, "col", masks[-1], masks[0])


def sum_rows(keep, send, count, rank, beside=None):
    x = keep + swap(send, "row", 1, 1)
    width = x.shape[1] - rank
    chunk = rank // count
    parts = [x[i * chunk:(i + 1) * chunk] for i in range(count // 2)]
    gram = jnp.concatenate([part[:, width:] for part in parts], axis=1)
    own = jnp.concatenate([parts[0][:, :width], gram], axis=1)
    gots = []
    for i in reversed(range(1, count // 2)):
        gots.append(swap(jnp.concatenate([parts[i][:, :width], gram], axis=1), "row", 2 * i, 2 * i))
    if beside is not None:
        gots[0], beside = lax.optimization_barrier((gots[0], beside))
    for got in gots:
        own = own + got
    own, gram = lax.optimization_barrier((own[:, :width], own[:, width:]))
    return own, gram, swap(gram, "row", 1, 1), beside


def gather_rows(x, count, meanwhile):
    own = [x] + [swap(x, "row", 2 * i, 2 * i) for i in range(1, count // 2)]
    done = meanwhile()
    other = [swap(x, "row", 1, 1)]
    for piece in own[1:]:
        piece, done = lax.optimization_barrier((piece, done))
        other.append(swap(piece, "row", 1, 1))
    return own, other, done


def shards(momentum, grad, basis):
    count = lax.axis_size("row")
    rank = basis.shape[1]
    rows, width = momentum.shape
    row_scale = float(rows * count) ** 0.5
    col_scale = float(width * lax.axis_size("col")) ** 0.5
    place = lax.axis_index("row").astype(jnp.int32).reshape(1)

    def left_side(one, two, before, beside=None):
        proj, turned, send = pull_send(count, place, one, two, high, low, before)
        keep = pull_keep(count, place, turned, proj, high, low, before)
        raw, own, other, beside = sum_rows(keep, send, count, rank, beside)
        first, second, inv = gather_rows(raw, count, lambda: factor_left(count, place, own, other))
        return left_of(proj, inv), inv, (first, second), beside

    high, low, proj = start(momentum, grad, basis)
    one, last_swap = sum_cols(proj)
    left_a, inv, pieces, _ = left_side(one, last_swap(one), None)
    right_a, image = normal(count, place, inv, *pieces, high, low)

    one, last_swap = sum_cols(image)
    gram, inv = factor_right(one, last_swap(one[rows:]), rows)
    two = last_swap(one[:rows])

    base = deflate(momentum, grad, left_a, right_a)
    left_b, inv, pieces, base = left_side(one, two, (left_a, right_a, gram, inv), base)
    right_b, gram = normal(count, place, inv, *pieces)

    gram, last_swap = sum_cols(gram)
    momentum_out, lefts = finish(base, left_b, right_b, left_a, row_scale)
    gram, momentum_out = lax.optimization_barrier((gram, momentum_out))
    momentum_out, = finish(base, left_b, right_b, momentum_out, part=1)
    turned = turn(right_b)
    return momentum_out, lefts, last_factor(gram, last_swap(gram), *turned, col_scale)


def solution(mesh):
    in_specs = (P("row", "col"), P("row", "col"), P("col", None))
    out_specs = (P("row", "col"), P(None, "row", None), P("col", None))
    return jax.shard_map(shards, mesh=mesh, in_specs=in_specs, out_specs=out_specs, check_vma=False)
```

```python
import jax
import jax.numpy as jnp
from jax import lax
from jax.experimental import pallas as pl
from jax.experimental.pallas import tpu as pltpu
from jax.sharding import PartitionSpec as P

F32 = jnp.float32
BF16 = jnp.bfloat16
HIGHEST = lax.Precision.HIGHEST
VMEM = pl.BlockSpec(memory_space=pltpu.VMEM)
SMEM = pl.BlockSpec(memory_space=pltpu.SMEM)
NN = (((1,), (0,)), ((), ()))
NT = (((1,), (1,)), ((), ()))
TN = (((0,), (0,)), ((), ()))
KEEP = 0.95
PANEL = 16
FACTOR = 1_500_000_000


def masks_of(axis):
    size = lax.axis_size(axis)
    masks = []
    mask = 1
    while mask < size:
        masks.append(mask)
        mask *= 2
    assert mask == size
    return masks


def swap(x, axis, even, odd):
    row_count, col_count = lax.axis_size("row"), lax.axis_size("col")
    pairs = []
    for row in range(row_count):
        mask = odd if row % 2 else even
        for col in range(col_count):
            to = (row ^ mask) * col_count + col if axis == "row" else row * col_count + (col ^ mask)
            pairs.append((row * col_count + col, to))
    return lax.ppermute(x, ("row", "col"), pairs)


def chunk_at(place, slot, other=False):
    return place ^ (2 * slot + (1 if other else 0))


def split(x):
    high = x.astype(BF16)
    return high, (x - high.astype(F32)).astype(BF16)


def dot(a, b, dims=NN):
    return lax.dot_general(a, b, dims, preferred_element_type=F32)


def exact(a, b, dims=NN):
    return lax.dot_general(a, b, dims, precision=HIGHEST, preferred_element_type=F32)


def parts3(a, b, dims=NN):
    a_high, a_low = split(a)
    b_high, b_low = split(b)
    return dot(a_high, b_high, dims) + (dot(a_low, b_high, dims) + dot(a_high, b_low, dims))


def tiles(width, most=256):
    return [(start, min(most, width - start)) for start in range(0, width, most)]


def struct(*shape, dtype=F32):
    return jax.ShapeDtypeStruct(shape, dtype)


def call(body, name, out, ins, scratch=(), flops=0, nbytes=0, **kw):
    return pl.pallas_call(
        body,
        out_shape=out,
        in_specs=[SMEM if x.dtype == jnp.int32 else VMEM for x in ins],
        out_specs=jax.tree.map(lambda _: VMEM, out),
        scratch_shapes=list(scratch),
        name=name,
        compiler_params=pltpu.CompilerParams(vmem_limit_bytes=24 * 2**20),
        cost_estimate=pl.CostEstimate(flops=flops, bytes_accessed=nbytes, transcendentals=0),
        **kw,
    )(*ins)


def start(momentum, grad, basis):
    rows, cols = momentum.shape
    rank = basis.shape[1]
    steps = 4
    block = rows // steps

    def body(momentum_hbm, grad_hbm, basis_hbm, high_ref, low_ref, top_ref, bottom_ref, momentum_ref, grad_ref, basis_ref, both_ref, sems):
        whole = pltpu.make_async_copy(basis_hbm, basis_ref, sems.at[0])
        whole.start()
        copies = []
        for i in range(steps):
            at = pl.ds(i * block, block)
            pair = (
                pltpu.make_async_copy(momentum_hbm.at[at], momentum_ref.at[at], sems.at[1 + 2 * i]),
                pltpu.make_async_copy(grad_hbm.at[at], grad_ref.at[at], sems.at[2 + 2 * i]),
            )
            for copy in pair:
                copy.start()
            copies.append(pair)
        whole.wait()
        high, low = split(basis_ref[...])
        both_ref[:, :rank] = high
        both_ref[:, rank:] = low
        for i in range(steps):
            for copy in copies[i]:
                copy.wait()
            at = pl.ds(i * block, block)
            high, low = split(momentum_ref[at, :] + grad_ref[at, :].astype(F32))
            high_ref[at, :] = high
            low_ref[at, :] = low
            wide = dot(high, both_ref[...])
            out_ref = top_ref if 2 * i < steps else bottom_ref
            at = pl.ds(i % (steps // 2) * block, block)
            out_ref[at, :] = wide[:, :rank] + wide[:, rank:] + dot(low, both_ref[:, :rank])

    return pl.pallas_call(
        body,
        in_specs=[pl.BlockSpec(memory_space=pltpu.HBM)] * 3,
        out_specs=[VMEM] * 4,
        out_shape=[struct(rows, cols, dtype=BF16)] * 2 + [struct(rows // 2, rank)] * 2,
        scratch_shapes=[
            pltpu.VMEM((rows, cols), F32),
            pltpu.VMEM((rows, cols), BF16),
            pltpu.VMEM((cols, rank), F32),
            pltpu.VMEM((cols, 2 * rank), BF16),
            pltpu.SemaphoreType.DMA((1 + 2 * steps,)),
        ],
        name="start",
        compiler_params=pltpu.CompilerParams(vmem_limit_bytes=24 * 2**20),
    )(*(pltpu.with_memory_space_constraint(x, pltpu.HBM) for x in (momentum, grad, basis)))


def pull_rows(turned, proj, high_ref, low_ref, cross, right_ref, out_ref):
    half = turned.shape[0]
    width = high_ref.shape[1]
    high, low = split(turned)
    both = jnp.concatenate([high, low], axis=0)
    for at, size in tiles(width):
        wide = dot(both, high_ref[:, at:at + size])
        out = wide[:half] + wide[half:] + dot(high, low_ref[:, at:at + size])
        if cross is not None:
            right_high, right_low = split(right_ref[:, at:at + size])
            wide = dot(jnp.concatenate(cross, axis=0), right_high)
            out = out + (wide[:half] + wide[half:] + dot(cross[0], right_low))
        out_ref[:, at:at + size] = out
    return gram_rows(high, low, both, proj)


def gram_rows(high, low, both, proj):
    half, rank = high.shape[0], proj.shape[1]
    proj_high, proj_low = split(proj)
    wide = dot(both, jnp.concatenate([proj_high, proj_low], axis=1))
    return wide[:half, :rank] + wide[:half, rank:] + wide[half:, :rank]


def put_gram(place, gram, out_ref, width, chunk):
    for t in range(gram.shape[0] // chunk):
        at = pl.multiple_of((place // 2 ^ t) * chunk, chunk)
        out_ref[pl.ds(at, chunk), width:] = gram[t * chunk:(t + 1) * chunk]


def pull_send(count, place, halves, high, low, before=None):
    rows, width = high.shape
    rank = halves[0].shape[1]
    chunk = rank // count
    skip = sum(x.shape[0] for x in halves[::2]) - rows

    def body(place_ref, a, b, c, d, high_ref, low_ref, *rest):
        place = place_ref[0]
        proj = jnp.concatenate([a[skip:, :] + b[skip:, :], c[...] + d[...]], axis=0)
        left_ref = right_ref = None
        if before is not None:
            left_ref, right_ref, gram_ref, inv_ref = rest[:4]
            proj = proj - KEEP * parts3(left_ref[...], gram_ref[...])
            proj = parts3(proj, inv_ref[...], NT)
        proj_ref, keep_ref, send_ref, turned_ref = rest[-4:]
        proj_ref[...] = proj
        turned_ref[...] = proj.T

        def pick(other):
            at = [chunk_at(place, t, other) * chunk for t in range(count // 2)]
            return jnp.concatenate([turned_ref[pl.ds(pl.multiple_of(x, chunk), chunk), :] for x in at], axis=0)

        keep_ref[...] = pick(False)
        turned = pick(True)
        cross = None if before is None else split(-KEEP * parts3(turned, left_ref[...]))
        gram = pull_rows(turned, proj, high_ref, low_ref, cross, right_ref, send_ref)
        put_gram(place, gram, send_ref, width, chunk)

    out = [struct(rows, rank), struct(rank // 2, rows), struct(rank // 2, width + rank)]
    ins = [place, *halves, high, low] + list(before or [])
    return call(body, "pull_send", out, ins, [pltpu.VMEM((rank, rows), F32)], flops=500_000_000, nbytes=5_000_000)


def pull_keep(count, place, turned, proj, high, low, before=None):
    rows, width = high.shape
    rank = proj.shape[1]
    chunk = rank // count

    def body(place_ref, turned_ref, proj_ref, high_ref, low_ref, *rest):
        place = place_ref[0]
        turned = turned_ref[...]
        cross = right_ref = None
        if before is not None:
            left_ref, right_ref = rest[:2]
            cross = split(-KEEP * parts3(turned, left_ref[...]))
        gram = pull_rows(turned, proj_ref[...], high_ref, low_ref, cross, right_ref, rest[-1])
        put_gram(place, gram, rest[-1], width, chunk)

    ins = [place, turned, proj, high, low] + list(before or [])[:2]
    return call(body, "pull_keep", struct(rank // 2, width + rank), ins, flops=500_000_000, nbytes=5_000_000)


def normal(count, place, inv, own, other, high=None, low=None):
    rank = inv.shape[0]
    width = own[0].shape[1]
    chunk = rank // count
    push = high is not None
    rows = high.shape[0] if push else 0
    cut = rank if push else 0

    def body(place_ref, inv_ref, *rest):
        pieces, rest = rest[:count], rest[count:]
        if push:
            work_high, work_low, right_ref, one_ref, two_ref, raw_ref = rest
        else:
            right_ref, one_ref, raw_ref = rest
        place = place_ref[0]
        for i, piece in enumerate(pieces):
            at = chunk_at(place, i % (count // 2), i >= count // 2) * chunk
            raw_ref[pl.ds(pl.multiple_of(at, chunk), chunk), :] = piece[...]
        inv_high, inv_low = split(inv_ref[...])
        inv_both = jnp.concatenate([inv_high, inv_low], axis=0)
        gram = jnp.zeros((rank, rank), F32)
        for at, size in tiles(width):
            raw_high, raw_low = split(raw_ref[:, at:at + size])
            wide = dot(inv_both, raw_high)
            right = wide[:rank] + wide[rank:] + dot(inv_high, raw_low)
            right_ref[:, at:at + size] = right
            high, low = split(right)
            both = jnp.concatenate([high, low], axis=0)
            wide = dot(both, high, NT)
            gram = gram + (wide[:rank] + wide[rank:] + dot(high, low, NT))
        one_ref[:rank, :] = gram
        if push:
            image = None
            for at, size in tiles(width):
                right_high, right_low = split(right_ref[:, at:at + size])
                wide = dot(work_high[:, at:at + size], jnp.concatenate([right_high, right_low], axis=0), NT)
                part = wide[:, :rank] + wide[:, rank:] + dot(work_low[:, at:at + size], right_high, NT)
                image = part if image is None else image + part
            one_ref[rank:, :] = image[:cut]
            two_ref[...] = image[cut:]

    ins = [place, inv, *own, *other] + ([high, low] if push else [])
    out = [struct(rank, width), struct(rank + cut, rank)] + ([struct(rows - cut, rank)] if push else [])
    return call(body, "normal", out, ins, [pltpu.VMEM((rank, width), F32)], flops=1_000_000_000, nbytes=5_000_000)


def left_of(proj, inv, before=None, scale=None):
    def body(proj_ref, inv_ref, *rest):
        left = parts3(proj_ref[...], inv_ref[...], NT)
        if before is None:
            rest[0][...] = left
        else:
            before_ref, left_ref, both_ref = rest
            left_ref[...] = left
            both_ref[0] = scale * before_ref[...]
            both_ref[1] = scale * left

    rows, rank = proj.shape
    if before is None:
        return call(body, "left", struct(rows, rank), [proj, inv], flops=100_000_000, nbytes=600_000)
    return call(body, "lefts", [struct(rows, rank), struct(2, rows, rank)], [proj, inv, before],
                flops=100_000_000, nbytes=1_200_000)


def outer_tile(left, right_high, right_low):
    high, low = split(left)
    rows = left.shape[0]
    wide = dot(jnp.concatenate([high, low], axis=0), right_high)
    return wide[:rows] + wide[rows:] + dot(high, right_low)


def deflate(momentum, grad, left, right):
    rows, cols = momentum.shape
    block = rows // 4

    def body(momentum_ref, grad_ref, left_ref, right_ref, out_ref):
        for at, size in tiles(cols):
            lanes = slice(at, at + size)
            right_high, right_low = split(KEEP * right_ref[:, lanes])
            for i in range(4):
                row = slice(i * block, (i + 1) * block)
                work = momentum_ref[row, lanes] + grad_ref[row, lanes].astype(F32)
                out_ref[row, lanes] = work - outer_tile(left_ref[row, :], right_high, right_low)

    return call(body, "deflate", struct(rows, cols), [momentum, grad, left, right], flops=1_500_000_000, nbytes=9_000_000)


def finish(base, left, right, before=None):
    rows, cols = base.shape
    rank = left.shape[1]
    half = rows // 2
    block = half // 2
    first = 0 if before is None else half

    def body(base_ref, left_ref, right_ref, *rest):
        out_ref, stage_ref, high_ref, low_ref, sems = rest[-5:]
        for at, size in tiles(cols):
            lanes = slice(at, at + size)
            high_ref[:, lanes], low_ref[:, lanes] = split(KEEP * right_ref[:, lanes])
        copies = []
        for i in range(2):
            row = slice(first + i * block, first + (i + 1) * block)
            for at, size in tiles(cols):
                lanes = slice(at, at + size)
                outer = outer_tile(left_ref[row, :], high_ref[:, lanes], low_ref[:, lanes])
                stage_ref[i, :, lanes] = base_ref[row, lanes] - outer
            copy = pltpu.make_async_copy(stage_ref.at[i], out_ref.at[pl.ds(first + i * block, block)], sems.at[i])
            copy.start()
            copies.append(copy)
        for copy in copies:
            copy.wait()

    hbm = pl.BlockSpec(memory_space=pltpu.HBM)
    more = [] if before is None else [before]
    return pl.pallas_call(
        body,
        in_specs=[VMEM] * 3 + [hbm] * len(more),
        out_specs=hbm,
        out_shape=struct(rows, cols),
        scratch_shapes=[pltpu.VMEM((2, block, cols), F32)] + [pltpu.VMEM((rank, cols), BF16)] * 2
        + [pltpu.SemaphoreType.DMA((2,))],
        input_output_aliases={3: 0} if more else {},
        name="finish",
        compiler_params=pltpu.CompilerParams(vmem_limit_bytes=24 * 2**20),
        cost_estimate=pl.CostEstimate(flops=800_000_000, bytes_accessed=6_000_000, transcendentals=0),
    )(base, left, right, *more)


def eliminate(full, first):
    rank = full.shape[1]
    groups = PANEL // 8
    sub = lax.broadcasted_iota(jnp.int32, (8, rank), 0)
    lane = lax.broadcasted_iota(jnp.int32, (8, rank), 1)
    rolled = pltpu.roll(full, lax.rem(rank - first, rank), 1)
    rows = [full[8 * g:8 * g + 8] for g in range(groups)]
    cols = [
        [jnp.broadcast_to(rolled[8 * g:8 * g + 8, j:j + 1], (8, rank)) for g in range(groups)] for j in range(PANEL)
    ]

    def spread(x, j):
        return jnp.broadcast_to(x[j // 8][j % 8:j % 8 + 1], (8, rank))

    pivot = spread(cols[0], 0)
    for j in range(PANEL):
        at = j // 8
        root = lax.rsqrt(pivot)
        if j + 1 < PANEL:
            above = spread(cols[j + 1], j) * root
            pivot = spread(cols[j + 1], j + 1) - above * above
        below = sub > j % 8
        here = lane == first + j
        row = jnp.where(here, 1.0, spread(rows, j)) * root
        for g in range(at, groups):
            mult = cols[j][g] * root
            rest = jnp.where(here, 0.0, rows[g])
            if g == at:
                mult = jnp.where(below, mult, 0.0)
                rest = jnp.where(below, rest, rows[g])
            rest = rest - mult * row
            rows[g] = jnp.where(sub == j % 8, row, rest) if g == at else rest
            cols[j][g] = mult
        for k in range(j + 1, PANEL):
            across = spread(cols[k], j) * root
            for g in range(at, groups):
                cols[k][g] = cols[k][g] - cols[j][g] * across
    return jnp.concatenate(rows, axis=0)


def thirds(x):
    high = x.astype(BF16)
    rest = x - high.astype(F32)
    middle = rest.astype(BF16)
    return high, middle, (rest - middle.astype(F32)).astype(BF16)


def factor_panels(state_ref):
    rank = state_ref.shape[0]
    row = lax.broadcasted_iota(jnp.int32, (rank, rank), 0)
    col = lax.broadcasted_iota(jnp.int32, (rank, rank), 1)
    sub = lax.broadcasted_iota(jnp.int32, (PANEL, rank), 0)
    lane = lax.broadcasted_iota(jnp.int32, (PANEL, rank), 1)

    def panel(p, carry):
        first = pl.multiple_of(p * PANEL, PANEL)
        done = eliminate(state_ref[pl.ds(first, PANEL), :], first)
        lower = jnp.where((lane > first + sub) & (lane < first + PANEL), 0.0, done)
        a, b, c = thirds(done)
        d, e, f = thirds(lower)
        step = dot(
            jnp.concatenate([a, a, b, b, a, c], axis=0), jnp.concatenate([d, e, d, e, f, d], axis=0), TN
        )
        old = state_ref[...]
        fresh = jnp.where((col >= first) & (col < first + PANEL), 0.0, old) - step
        state_ref[...] = jnp.where(row >= first + PANEL, fresh, old)
        state_ref[pl.ds(first, PANEL), :] = done
        return carry

    lax.fori_loop(0, rank // PANEL, panel, 0)


def factor_left(count, place, own, other):
    chunk, rank = own.shape[0], 2 * own.shape[1] // count

    def body(place_ref, own_ref, other_ref, out_ref):
        core = place_ref[0] % 2
        for t in range(count // 2):
            for ref, at in ((own_ref, 2 * t + core), (other_ref, 2 * t + 1 - core)):
                out_ref[pl.ds(pl.multiple_of(at * chunk, chunk), chunk), :] = ref[:, t * rank:(t + 1) * rank]
        factor_panels(out_ref)
        out_ref[...] = lower_part(out_ref[...])

    return call(body, "factor", struct(rank, rank), [place, own, other], flops=2 * FACTOR, nbytes=131072)


def factor_right(one, two):
    rank = one.shape[1]

    def body(one_ref, two_ref, gram_ref, out_ref):
        gram = one_ref[:rank, :] + two_ref[:rank, :]
        gram_ref[...] = gram
        out_ref[...] = gram
        factor_panels(out_ref)
        out_ref[...] = lower_part(out_ref[...])

    return call(body, "factor", [struct(rank, rank)] * 2, [one, two], flops=2 * FACTOR, nbytes=131072)


def lower_part(x):
    row = lax.broadcasted_iota(jnp.int32, x.shape, 0)
    col = lax.broadcasted_iota(jnp.int32, x.shape, 1)
    return jnp.where(row >= col, x, 0.0)


def turn(right):
    rank, width = right.shape

    def body(right_ref, high_ref, low_ref):
        high, low = split(right_ref[...].T)
        high_ref[...] = high
        low_ref[...] = low

    return call(body, "turn", [struct(width, rank, dtype=BF16)] * 2, [right], flops=100_000_000, nbytes=2_000_000)


def last_factor(one, two, high, low, scale):
    def body(one_ref, two_ref, high_ref, low_ref, out_ref, state_ref):
        rank = state_ref.shape[0]
        state_ref[...] = one_ref[...] + two_ref[...]
        factor_panels(state_ref)
        inv_high, inv_low = split(scale * lower_part(state_ref[...]))
        both = jnp.concatenate([inv_high, inv_low], axis=0)
        wide = dot(high_ref[...], both, NT)
        out_ref[...] = wide[:, :rank] + wide[:, rank:] + dot(low_ref[...], inv_high, NT)

    width, rank = high.shape
    return call(body, "last_factor", struct(width, rank), [one, two, high, low], [pltpu.VMEM((rank, rank), F32)],
                flops=2 * FACTOR, nbytes=2_000_000)


def sum_cols(parts):
    masks = masks_of("col")
    for even, odd in zip(masks[:-1], masks[:0:-1]):
        parts = [x + swap(x, "col", even, odd) for x in parts]
    return [y for x in parts for y in (x, swap(x, "col", masks[-1], masks[0]))]


def sum_rows(keep, send, count, rank, beside=None):
    x = keep + swap(send, "row", 1, 1)
    if beside is not None:
        work, seed = beside
        x, seed = lax.optimization_barrier((x, seed))
        beside = work(seed)
    width = x.shape[1] - rank
    chunk = rank // count
    slots = count // 2
    cut = width // rank // 2 * rank
    cut = width - cut
    parts = [x[i * chunk:(i + 1) * chunk] for i in range(slots)]
    gram = jnp.concatenate([part[:, width:] for part in parts], axis=1)
    stepped = {i: part[:, cut:width] for i, part in enumerate(parts)}
    own = parts[0][:, :cut]
    straight = {}
    bit = 1
    while bit < slots:
        sent = [i for i in stepped if i & bit]
        kept = [i for i in stepped if not i & bit]
        cols = [stepped[i] for i in sent] + [gram]
        first = [parts[1][:, :cut]] if bit == 1 else []
        got = swap(jnp.concatenate(first + cols, axis=1), "row", 2 * bit, 2 * bit)
        if bit == 1:
            straight[1], got = got[:, :cut], got[:, cut:]
            for i in reversed(range(2, slots)):
                straight[i] = swap(parts[i][:, :cut], "row", 2 * i, 2 * i)
            if beside is not None:
                got, beside = lax.optimization_barrier((got, beside))
        size = width - cut
        stepped = {i: stepped[i] + got[:, n * size:(n + 1) * size] for n, i in enumerate(kept)}
        gram = gram + got[:, len(kept) * size:]
        bit *= 2
    for i in straight:
        own = own + straight[i]
    own = jnp.concatenate([own, stepped[0]], axis=1)
    own, gram = lax.optimization_barrier((own, gram))
    return own, gram, swap(gram, "row", 1, 1), beside


def gather_rows(x, count, meanwhile):
    own = [x] + [swap(x, "row", 2 * i, 2 * i) for i in range(1, count // 2)]
    done = meanwhile()
    other = [swap(x, "row", 1, 1)]
    for piece in own[1:]:
        piece, done = lax.optimization_barrier((piece, done))
        other.append(swap(piece, "row", 1, 1))
    return own, other, done


def shards(momentum, grad, basis):
    count = lax.axis_size("row")
    rank = basis.shape[1]
    rows, width = momentum.shape
    row_scale = float(rows * count) ** 0.5
    col_scale = float(width * lax.axis_size("col")) ** 0.5
    place = lax.axis_index("row").astype(jnp.int32).reshape(1)

    def left_side(halves, before=None, beside=None):
        proj, turned, send = pull_send(count, place, halves, high, low, before)
        keep = pull_keep(count, place, turned, proj, high, low, before)
        raw, own, other, beside = sum_rows(keep, send, count, rank, beside)
        first, second, inv = gather_rows(raw, count, lambda: factor_left(count, place, own, other))
        return proj, inv, (first, second), beside

    high, low, *parts = start(momentum, grad, basis)
    proj, inv, pieces, _ = left_side(sum_cols(parts))
    left_a = left_of(proj, inv)
    right_a, *parts = normal(count, place, inv, *pieces, high, low)

    halves = sum_cols(parts)
    gram, inv = factor_right(*halves[:2])

    beside = (lambda left: deflate(momentum, grad, left, right_a)), left_a
    proj, inv, pieces, base = left_side(halves, (left_a, right_a, gram, inv), beside)
    left_b, lefts = left_of(proj, inv, left_a, row_scale)
    right_b, gram = normal(count, place, inv, *pieces)

    masks = masks_of("col")
    momentum_out = finish(base, left_b, right_b)
    for even, odd in zip(masks[:-1], masks[:0:-1]):
        gram = gram + swap(gram, "col", even, odd)
    gram, momentum_out = lax.optimization_barrier((gram, momentum_out))
    momentum_out = finish(base, left_b, right_b, momentum_out)
    turned = turn(right_b)
    return momentum_out, lefts, last_factor(gram, swap(gram, "col", masks[-1], masks[0]), *turned, col_scale)


def solution(mesh):
    in_specs = (P("row", "col"), P("row", "col"), P("col", None))
    out_specs = (P("row", "col"), P(None, "row", None), P("col", None))
    return jax.shard_map(shards, mesh=mesh, in_specs=in_specs, out_specs=out_specs, check_vma=False)
```

```python
import jax
import jax.numpy as jnp
from jax import lax
from jax.experimental import pallas as pl
from jax.experimental.pallas import tpu as pltpu
from jax.sharding import PartitionSpec as P

F32 = jnp.float32
BF16 = jnp.bfloat16
HIGHEST = lax.Precision.HIGHEST
VMEM = pl.BlockSpec(memory_space=pltpu.VMEM)
SMEM = pl.BlockSpec(memory_space=pltpu.SMEM)
NN = (((1,), (0,)), ((), ()))
NT = (((1,), (1,)), ((), ()))
TN = (((0,), (0,)), ((), ()))
KEEP = 0.95
PANEL = 16
FACTOR = 20_000_000_000


def masks_of(axis):
    size = lax.axis_size(axis)
    masks = []
    mask = 1
    while mask < size:
        masks.append(mask)
        mask *= 2
    assert mask == size
    return masks


def swap(x, axis, even, odd):
    row_count, col_count = lax.axis_size("row"), lax.axis_size("col")
    pairs = []
    for row in range(row_count):
        mask = odd if row % 2 else even
        for col in range(col_count):
            to = (row ^ mask) * col_count + col if axis == "row" else row * col_count + (col ^ mask)
            pairs.append((row * col_count + col, to))
    return lax.ppermute(x, ("row", "col"), pairs)


def chunk_at(place, slot, other=False):
    return place ^ (2 * slot + (1 if other else 0))


def split(x):
    high = x.astype(BF16)
    return high, (x - high.astype(F32)).astype(BF16)


def dot(a, b, dims=NN):
    return lax.dot_general(a, b, dims, preferred_element_type=F32)


def exact(a, b, dims=NN):
    return lax.dot_general(a, b, dims, precision=HIGHEST, preferred_element_type=F32)


def parts3(a, b, dims=NN):
    a_high, a_low = split(a)
    b_high, b_low = split(b)
    return dot(a_high, b_high, dims) + (dot(a_low, b_high, dims) + dot(a_high, b_low, dims))


def tiles(width, most=256):
    return [(start, min(most, width - start)) for start in range(0, width, most)]


def struct(*shape, dtype=F32):
    return jax.ShapeDtypeStruct(shape, dtype)


def call(body, name, out, ins, scratch=(), flops=0, nbytes=0, **kw):
    return pl.pallas_call(
        body,
        out_shape=out,
        in_specs=[SMEM if x.dtype == jnp.int32 else VMEM for x in ins],
        out_specs=jax.tree.map(lambda _: VMEM, out),
        scratch_shapes=list(scratch),
        name=name,
        compiler_params=pltpu.CompilerParams(vmem_limit_bytes=24 * 2**20),
        cost_estimate=pl.CostEstimate(flops=flops, bytes_accessed=nbytes, transcendentals=0),
        **kw,
    )(*ins)


def start(momentum, grad, basis):
    rows, cols = momentum.shape
    rank = basis.shape[1]
    steps = 4
    block = rows // steps

    def body(momentum_hbm, grad_hbm, basis_hbm, high_ref, low_ref, top_ref, bottom_ref, momentum_ref, grad_ref, basis_ref, both_ref, sems):
        whole = pltpu.make_async_copy(basis_hbm, basis_ref, sems.at[0])
        whole.start()
        copies = []
        for i in range(steps):
            at = pl.ds(i * block, block)
            pair = (
                pltpu.make_async_copy(momentum_hbm.at[at], momentum_ref.at[at], sems.at[1 + 2 * i]),
                pltpu.make_async_copy(grad_hbm.at[at], grad_ref.at[at], sems.at[2 + 2 * i]),
            )
            for copy in pair:
                copy.start()
            copies.append(pair)
        whole.wait()
        high, low = split(basis_ref[...])
        both_ref[:, :rank] = high
        both_ref[:, rank:] = low
        for i in range(steps):
            for copy in copies[i]:
                copy.wait()
            at = pl.ds(i * block, block)
            high, low = split(momentum_ref[at, :] + grad_ref[at, :].astype(F32))
            high_ref[at, :] = high
            low_ref[at, :] = low
            wide = dot(high, both_ref[...])
            out_ref = top_ref if 2 * i < steps else bottom_ref
            at = pl.ds(i % (steps // 2) * block, block)
            out_ref[at, :] = wide[:, :rank] + wide[:, rank:] + dot(low, both_ref[:, :rank])

    return pl.pallas_call(
        body,
        in_specs=[pl.BlockSpec(memory_space=pltpu.HBM)] * 3,
        out_specs=[VMEM] * 4,
        out_shape=[struct(rows, cols, dtype=BF16)] * 2 + [struct(rows // 2, rank)] * 2,
        scratch_shapes=[
            pltpu.VMEM((rows, cols), F32),
            pltpu.VMEM((rows, cols), BF16),
            pltpu.VMEM((cols, rank), F32),
            pltpu.VMEM((cols, 2 * rank), BF16),
            pltpu.SemaphoreType.DMA((1 + 2 * steps,)),
        ],
        name="start",
        compiler_params=pltpu.CompilerParams(vmem_limit_bytes=24 * 2**20),
    )(*(pltpu.with_memory_space_constraint(x, pltpu.HBM) for x in (momentum, grad, basis)))


def pull_rows(turned, proj, high_ref, low_ref, cross, right_ref, out_ref):
    half = turned.shape[0]
    width = high_ref.shape[1]
    high, low = split(turned)
    both = jnp.concatenate([high, low], axis=0)
    for at, size in tiles(width):
        wide = dot(both, high_ref[:, at:at + size])
        out = wide[:half] + wide[half:] + dot(high, low_ref[:, at:at + size])
        if cross is not None:
            right_high, right_low = split(right_ref[:, at:at + size])
            wide = dot(jnp.concatenate(cross, axis=0), right_high)
            out = out + (wide[:half] + wide[half:] + dot(cross[0], right_low))
        out_ref[:, at:at + size] = out
    return gram_rows(high, low, both, proj)


def gram_rows(high, low, both, proj):
    half, rank = high.shape[0], proj.shape[1]
    proj_high, proj_low = split(proj)
    wide = dot(both, jnp.concatenate([proj_high, proj_low], axis=1))
    return wide[:half, :rank] + wide[:half, rank:] + wide[half:, :rank]


def put_gram(place, gram, out_ref, width, chunk):
    for t in range(gram.shape[0] // chunk):
        at = pl.multiple_of((place // 2 ^ t) * chunk, chunk)
        out_ref[pl.ds(at, chunk), width:] = gram[t * chunk:(t + 1) * chunk]


def pull_send(count, place, halves, high, low, before=None):
    rows, width = high.shape
    rank = halves[0].shape[1]
    chunk = rank // count

    pairs = len(halves)

    def body(place_ref, *rest):
        place = place_ref[0]
        sums = [one[...] + two[...] for one, two in zip(rest[0:pairs:2], rest[1:pairs:2])]
        proj = jnp.concatenate(sums, axis=0)
        high_ref, low_ref, *rest = rest[pairs:]
        left_ref = right_ref = None
        if before is not None:
            left_ref, right_ref, gram_ref, inv_ref = rest[:4]
            proj = proj - KEEP * parts3(left_ref[...], gram_ref[...])
            proj = parts3(proj, inv_ref[...], NT)
        proj_ref, keep_ref, send_ref, turned_ref = rest[-4:]
        proj_ref[...] = proj
        turned_ref[...] = proj.T

        def pick(other):
            at = [chunk_at(place, t, other) * chunk for t in range(count // 2)]
            return jnp.concatenate([turned_ref[pl.ds(pl.multiple_of(x, chunk), chunk), :] for x in at], axis=0)

        keep_ref[...] = pick(False)
        turned = pick(True)
        cross = None if before is None else split(-KEEP * parts3(turned, left_ref[...]))
        gram = pull_rows(turned, proj, high_ref, low_ref, cross, right_ref, send_ref)
        put_gram(place, gram, send_ref, width, chunk)

    out = [struct(rows, rank), struct(rank // 2, rows), struct(rank // 2, width + rank)]
    ins = [place, *halves, high, low] + list(before or [])
    return call(body, "pull_send", out, ins, [pltpu.VMEM((rank, rows), F32)], flops=500_000_000, nbytes=5_000_000)


def pull_keep(count, place, turned, proj, high, low, before=None):
    rows, width = high.shape
    rank = proj.shape[1]
    chunk = rank // count

    def body(place_ref, turned_ref, proj_ref, high_ref, low_ref, *rest):
        place = place_ref[0]
        turned = turned_ref[...]
        cross = right_ref = None
        if before is not None:
            left_ref, right_ref = rest[:2]
            cross = split(-KEEP * parts3(turned, left_ref[...]))
        gram = pull_rows(turned, proj_ref[...], high_ref, low_ref, cross, right_ref, rest[-1])
        put_gram(place, gram, rest[-1], width, chunk)

    ins = [place, turned, proj, high, low] + list(before or [])[:2]
    return call(body, "pull_keep", struct(rank // 2, width + rank), ins, flops=500_000_000, nbytes=5_000_000)


def normal(count, place, inv, own, other):
    rank = inv.shape[0]
    width = own[0].shape[1]
    chunk = rank // count

    def body(place_ref, inv_ref, *rest):
        pieces = rest[:count]
        right_ref, gram_ref, raw_ref = rest[count:]
        place = place_ref[0]
        for i, piece in enumerate(pieces):
            at = chunk_at(place, i % (count // 2), i >= count // 2) * chunk
            raw_ref[pl.ds(pl.multiple_of(at, chunk), chunk), :] = piece[...]
        inv_high, inv_low = split(inv_ref[...])
        inv_both = jnp.concatenate([inv_high, inv_low], axis=0)
        gram = jnp.zeros((rank, rank), F32)
        for at, size in tiles(width):
            raw_high, raw_low = split(raw_ref[:, at:at + size])
            wide = dot(inv_both, raw_high)
            right = wide[:rank] + wide[rank:] + dot(inv_high, raw_low)
            right_ref[:, at:at + size] = right
            high, low = split(right)
            wide = dot(jnp.concatenate([high, low], axis=0), high, NT)
            gram = gram + (wide[:rank] + wide[rank:] + dot(high, low, NT))
        gram_ref[...] = gram

    return call(body, "normal", [struct(rank, width), struct(rank, rank)], [place, inv, *own, *other],
                [pltpu.VMEM((rank, width), F32)], flops=500_000_000, nbytes=2_000_000)


def push(high, low, right):
    rows, width = high.shape
    rank = right.shape[0]

    def body(high_ref, low_ref, right_ref, out_ref):
        image = None
        for at, size in tiles(width):
            right_high, right_low = split(right_ref[:, at:at + size])
            wide = dot(high_ref[:, at:at + size], jnp.concatenate([right_high, right_low], axis=0), NT)
            part = wide[:, :rank] + wide[:, rank:] + dot(low_ref[:, at:at + size], right_high, NT)
            image = part if image is None else image + part
        out_ref[...] = image

    return call(body, "push", struct(rows, rank), [high, low, right], flops=1_000_000_000, nbytes=5_000_000)


def left_of(proj, inv, before=None, scale=None):
    def body(proj_ref, inv_ref, *rest):
        left = parts3(proj_ref[...], inv_ref[...], NT)
        if before is None:
            rest[0][...] = left
        else:
            before_ref, left_ref, both_ref = rest
            left_ref[...] = left
            both_ref[0] = scale * before_ref[...]
            both_ref[1] = scale * left

    rows, rank = proj.shape
    if before is None:
        return call(body, "left", struct(rows, rank), [proj, inv], flops=100_000_000, nbytes=600_000)
    return call(body, "lefts", [struct(rows, rank), struct(2, rows, rank)], [proj, inv, before],
                flops=100_000_000, nbytes=1_200_000)


def outer_tile(left, right_high, right_low):
    high, low = split(left)
    rows = left.shape[0]
    wide = dot(jnp.concatenate([high, low], axis=0), right_high)
    return wide[:rows] + wide[rows:] + dot(high, right_low)


def deflate(momentum, grad, left, right):
    rows, cols = momentum.shape
    block = rows // 4

    def body(momentum_ref, grad_ref, left_ref, right_ref, out_ref):
        for at, size in tiles(cols):
            lanes = slice(at, at + size)
            right_high, right_low = split(KEEP * right_ref[:, lanes])
            for i in range(4):
                row = slice(i * block, (i + 1) * block)
                work = momentum_ref[row, lanes] + grad_ref[row, lanes].astype(F32)
                out_ref[row, lanes] = work - outer_tile(left_ref[row, :], right_high, right_low)

    return call(body, "deflate", struct(rows, cols), [momentum, grad, left, right], flops=1_500_000_000, nbytes=9_000_000)


def finish(base, left, right, before=None):
    rows, cols = base.shape
    rank = left.shape[1]
    half = rows // 2
    block = half // 2
    first = 0 if before is None else half

    def body(base_ref, left_ref, right_ref, *rest):
        out_ref, stage_ref, high_ref, low_ref, sems = rest[-5:]
        for at, size in tiles(cols):
            lanes = slice(at, at + size)
            high_ref[:, lanes], low_ref[:, lanes] = split(KEEP * right_ref[:, lanes])
        copies = []
        for i in range(2):
            row = slice(first + i * block, first + (i + 1) * block)
            for at, size in tiles(cols):
                lanes = slice(at, at + size)
                outer = outer_tile(left_ref[row, :], high_ref[:, lanes], low_ref[:, lanes])
                stage_ref[i, :, lanes] = base_ref[row, lanes] - outer
            copy = pltpu.make_async_copy(stage_ref.at[i], out_ref.at[pl.ds(first + i * block, block)], sems.at[i])
            copy.start()
            copies.append(copy)
        for copy in copies:
            copy.wait()

    hbm = pl.BlockSpec(memory_space=pltpu.HBM)
    more = [] if before is None else [before]
    return pl.pallas_call(
        body,
        in_specs=[VMEM] * 3 + [hbm] * len(more),
        out_specs=hbm,
        out_shape=struct(rows, cols),
        scratch_shapes=[pltpu.VMEM((2, block, cols), F32)] + [pltpu.VMEM((rank, cols), BF16)] * 2
        + [pltpu.SemaphoreType.DMA((2,))],
        input_output_aliases={3: 0} if more else {},
        name="finish",
        compiler_params=pltpu.CompilerParams(vmem_limit_bytes=24 * 2**20),
        cost_estimate=pl.CostEstimate(flops=800_000_000, bytes_accessed=6_000_000, transcendentals=0),
    )(base, left, right, *more)


def eliminate(full, first, size):
    rank = full.shape[1]
    groups = size // 8
    sub = lax.broadcasted_iota(jnp.int32, (8, rank), 0)
    lane = lax.broadcasted_iota(jnp.int32, (8, rank), 1)
    rolled = pltpu.roll(full, lax.rem(rank - first, rank), 1)
    rows = [full[8 * g:8 * g + 8] for g in range(groups)]
    cols = [
        [jnp.broadcast_to(rolled[8 * g:8 * g + 8, j:j + 1], (8, rank)) for g in range(groups)] for j in range(size)
    ]

    def spread(x, j):
        return jnp.broadcast_to(x[j // 8][j % 8:j % 8 + 1], (8, rank))

    pivot = spread(cols[0], 0)
    for j in range(size):
        at = j // 8
        root = lax.rsqrt(pivot)
        if j + 1 < size:
            above = spread(cols[j + 1], j) * root
            pivot = spread(cols[j + 1], j + 1) - above * above
        below = sub > j % 8
        here = lane == first + j
        row = jnp.where(here, 1.0, spread(rows, j)) * root
        for g in range(at, groups):
            mult = cols[j][g] * root
            rest = jnp.where(here, 0.0, rows[g])
            if g == at:
                mult = jnp.where(below, mult, 0.0)
                rest = jnp.where(below, rest, rows[g])
            rest = rest - mult * row
            rows[g] = jnp.where(sub == j % 8, row, rest) if g == at else rest
            cols[j][g] = mult
        for k in range(j + 1, size):
            across = spread(cols[k], j) * root
            for g in range(at, groups):
                cols[k][g] = cols[k][g] - cols[j][g] * across
    return jnp.concatenate(rows, axis=0)


def thirds(x):
    high = x.astype(BF16)
    rest = x - high.astype(F32)
    middle = rest.astype(BF16)
    return high, middle, (rest - middle.astype(F32)).astype(BF16)


def factor_panels(state_ref, size=PANEL):
    rank = state_ref.shape[0]
    row = lax.broadcasted_iota(jnp.int32, (rank, rank), 0)
    col = lax.broadcasted_iota(jnp.int32, (rank, rank), 1)
    sub = lax.broadcasted_iota(jnp.int32, (size, rank), 0)
    lane = lax.broadcasted_iota(jnp.int32, (size, rank), 1)

    def panel(p, carry):
        first = pl.multiple_of(p * size, size)
        done = eliminate(state_ref[pl.ds(first, size), :], first, size)
        lower = jnp.where((lane > first + sub) & (lane < first + size), 0.0, done)
        a, b, c = thirds(done)
        d, e, f = thirds(lower)
        step = dot(
            jnp.concatenate([a, a, b, b, a, c], axis=0), jnp.concatenate([d, e, d, e, f, d], axis=0), TN
        )
        old = state_ref[...]
        fresh = jnp.where((col >= first) & (col < first + size), 0.0, old) - step
        state_ref[...] = jnp.where(row >= first + size, fresh, old)
        state_ref[pl.ds(first, size), :] = done
        return carry

    lax.fori_loop(0, rank // size, panel, 0)


def factor_left(count, place, own, other):
    chunk, rank = own.shape[0], 2 * own.shape[1] // count

    def body(place_ref, own_ref, other_ref, out_ref):
        core = place_ref[0] % 2
        for t in range(count // 2):
            for ref, at in ((own_ref, 2 * t + core), (other_ref, 2 * t + 1 - core)):
                out_ref[pl.ds(pl.multiple_of(at * chunk, chunk), chunk), :] = ref[:, t * rank:(t + 1) * rank]
        factor_panels(out_ref, 32)
        out_ref[...] = lower_part(out_ref[...])

    return call(body, "factor", struct(rank, rank), [place, own, other], flops=2 * FACTOR, nbytes=131072)


def factor_right(one, two):
    rank = one.shape[1]

    def body(one_ref, two_ref, gram_ref, out_ref):
        gram = one_ref[:rank, :] + two_ref[:rank, :]
        gram_ref[...] = gram
        out_ref[...] = gram
        factor_panels(out_ref)
        out_ref[...] = lower_part(out_ref[...])

    return call(body, "factor", [struct(rank, rank)] * 2, [one, two], flops=2 * FACTOR, nbytes=131072)


def lower_part(x):
    row = lax.broadcasted_iota(jnp.int32, x.shape, 0)
    col = lax.broadcasted_iota(jnp.int32, x.shape, 1)
    return jnp.where(row >= col, x, 0.0)


def turn(right):
    rank, width = right.shape

    def body(right_ref, high_ref, low_ref):
        high, low = split(right_ref[...].T)
        high_ref[...] = high
        low_ref[...] = low

    return call(body, "turn", [struct(width, rank, dtype=BF16)] * 2, [right], flops=100_000_000, nbytes=2_000_000)


def last_factor(one, two, high, low, scale):
    width, rank = high.shape
    steps = 4
    block = width // steps

    def body(one_ref, two_ref, high_ref, low_ref, out_ref, state_ref, stage_ref, sems):
        state_ref[...] = one_ref[...] + two_ref[...]
        factor_panels(state_ref)
        inv_high, inv_low = split(scale * lower_part(state_ref[...]))
        both = jnp.concatenate([inv_high, inv_low], axis=0)
        copies = []
        for i in range(steps):
            row = slice(i * block, (i + 1) * block)
            wide = dot(high_ref[row, :], both, NT)
            stage_ref[row, :] = wide[:, :rank] + wide[:, rank:] + dot(low_ref[row, :], inv_high, NT)
            at = pl.ds(i * block, block)
            copy = pltpu.make_async_copy(stage_ref.at[at], out_ref.at[at], sems.at[i])
            copy.start()
            copies.append(copy)
        for copy in copies:
            copy.wait()

    return pl.pallas_call(
        body,
        in_specs=[VMEM] * 4,
        out_specs=pl.BlockSpec(memory_space=pltpu.HBM),
        out_shape=struct(width, rank),
        scratch_shapes=[pltpu.VMEM((rank, rank), F32), pltpu.VMEM((width, rank), F32), pltpu.SemaphoreType.DMA((steps,))],
        name="last_factor",
        compiler_params=pltpu.CompilerParams(vmem_limit_bytes=24 * 2**20),
        cost_estimate=pl.CostEstimate(flops=2 * FACTOR, bytes_accessed=2_000_000, transcendentals=0),
    )(one, two, high, low)


def sum_cols(parts):
    masks = masks_of("col")
    for even, odd in zip(masks[:-1], masks[:0:-1]):
        parts = [x + swap(x, "col", even, odd) for x in parts]
    return [y for x in parts for y in (x, swap(x, "col", masks[-1], masks[0]))]


def sum_rows(keep, send, count, rank, beside=None):
    x = keep + swap(send, "row", 1, 1)
    if beside is not None:
        work, seed = beside
        x, seed = lax.optimization_barrier((x, seed))
        beside = work(seed)
    width = x.shape[1] - rank
    chunk = rank // count
    slots = count // 2
    parts = [x[i * chunk:(i + 1) * chunk] for i in range(slots)]
    gram = jnp.concatenate([part[:, width:] for part in parts], axis=1)
    got = swap(jnp.concatenate([parts[1][:, :width], gram], axis=1), "row", 2, 2)
    gots = [swap(parts[i][:, :width], "row", 2 * i, 2 * i) for i in range(2, slots)]
    gram = gram + got[:, width:]
    if beside is not None:
        gram, beside = lax.optimization_barrier((gram, beside))
    for mask in masks_of("row")[2:]:
        gram = gram + swap(gram, "row", mask, mask)
    own = parts[0][:, :width] + got[:, :width]
    for got in gots:
        own = own + got
    own, gram = lax.optimization_barrier((own, gram))
    return own, gram, swap(gram, "row", 1, 1), beside


def gather_rows(x, count, meanwhile):
    own = [x] + [swap(x, "row", 2 * i, 2 * i) for i in range(1, count // 2)]
    done = meanwhile()
    other = [swap(x, "row", 1, 1)]
    for piece in own[1:]:
        piece, done = lax.optimization_barrier((piece, done))
        other.append(swap(piece, "row", 1, 1))
    return own, other, done


def shards(momentum, grad, basis):
    count = lax.axis_size("row")
    rank = basis.shape[1]
    rows, width = momentum.shape
    row_scale = float(rows * count) ** 0.5
    col_scale = float(width * lax.axis_size("col")) ** 0.5
    place = lax.axis_index("row").astype(jnp.int32).reshape(1)

    def left_side(halves, before=None, beside=None):
        proj, turned, send = pull_send(count, place, halves, high, low, before)
        keep = pull_keep(count, place, turned, proj, high, low, before)
        raw, own, other, beside = sum_rows(keep, send, count, rank, beside)
        first, second, inv = gather_rows(raw, count, lambda: factor_left(count, place, own, other))
        return proj, inv, (first, second), beside

    high, low, *parts = start(momentum, grad, basis)
    proj, inv, pieces, _ = left_side(sum_cols(parts))
    left_a = left_of(proj, inv)
    right_a, gram = normal(count, place, inv, *pieces)
    gram, inv = factor_right(*sum_cols([gram]))
    halves = sum_cols([push(high, low, right_a)])

    beside = (lambda left: deflate(momentum, grad, left, right_a)), left_a
    proj, inv, pieces, base = left_side(halves, (left_a, right_a, gram, inv), beside)
    left_b, lefts = left_of(proj, inv, left_a, row_scale)
    right_b, gram = normal(count, place, inv, *pieces)

    masks = masks_of("col")
    momentum_out = finish(base, left_b, right_b)
    for even, odd in zip(masks[:-1], masks[:0:-1]):
        gram = gram + swap(gram, "col", even, odd)
    gram, momentum_out = lax.optimization_barrier((gram, momentum_out))
    momentum_out = finish(base, left_b, right_b, momentum_out)
    turned = turn(right_b)
    return momentum_out, lefts, last_factor(gram, swap(gram, "col", masks[-1], masks[0]), *turned, col_scale)


def solution(mesh):
    in_specs = (P("row", "col"), P("row", "col"), P("col", None))
    out_specs = (P("row", "col"), P(None, "row", None), P("col", None))
    return jax.shard_map(shards, mesh=mesh, in_specs=in_specs, out_specs=out_specs, check_vma=False)
```

```python
import jax
import jax.numpy as jnp
from jax import lax
from jax.experimental import pallas as pl
from jax.experimental.pallas import tpu as pltpu
from jax.sharding import PartitionSpec as P

F32 = jnp.float32
BF16 = jnp.bfloat16
HIGHEST = lax.Precision.HIGHEST
VMEM = pl.BlockSpec(memory_space=pltpu.VMEM)
SMEM = pl.BlockSpec(memory_space=pltpu.SMEM)
NN = (((1,), (0,)), ((), ()))
NT = (((1,), (1,)), ((), ()))
TN = (((0,), (0,)), ((), ()))
KEEP = 0.95
PANEL = 16
FACTOR = 20_000_000_000


def masks_of(axis):
    size = lax.axis_size(axis)
    masks = []
    mask = 1
    while mask < size:
        masks.append(mask)
        mask *= 2
    assert mask == size
    return masks


def swap(x, axis, even, odd):
    row_count, col_count = lax.axis_size("row"), lax.axis_size("col")
    pairs = []
    for row in range(row_count):
        mask = odd if row % 2 else even
        for col in range(col_count):
            to = (row ^ mask) * col_count + col if axis == "row" else row * col_count + (col ^ mask)
            pairs.append((row * col_count + col, to))
    return lax.ppermute(x, ("row", "col"), pairs)


def chunk_at(place, slot, other=False):
    return place ^ (2 * slot + (1 if other else 0))


def split(x):
    high = x.astype(BF16)
    return high, (x - high.astype(F32)).astype(BF16)


def dot(a, b, dims=NN):
    return lax.dot_general(a, b, dims, preferred_element_type=F32)


def exact(a, b, dims=NN):
    return lax.dot_general(a, b, dims, precision=HIGHEST, preferred_element_type=F32)


def parts3(a, b, dims=NN):
    a_high, a_low = split(a)
    b_high, b_low = split(b)
    return dot(a_high, b_high, dims) + (dot(a_low, b_high, dims) + dot(a_high, b_low, dims))


def tiles(width, most=256):
    return [(start, min(most, width - start)) for start in range(0, width, most)]


def struct(*shape, dtype=F32):
    return jax.ShapeDtypeStruct(shape, dtype)


def call(body, name, out, ins, scratch=(), flops=0, nbytes=0, **kw):
    return pl.pallas_call(
        body,
        out_shape=out,
        in_specs=[SMEM if x.dtype == jnp.int32 else VMEM for x in ins],
        out_specs=jax.tree.map(lambda _: VMEM, out),
        scratch_shapes=list(scratch),
        name=name,
        compiler_params=pltpu.CompilerParams(vmem_limit_bytes=24 * 2**20),
        cost_estimate=pl.CostEstimate(flops=flops, bytes_accessed=nbytes, transcendentals=0),
        **kw,
    )(*ins)


def start(momentum, grad, basis):
    rows, cols = momentum.shape
    rank = basis.shape[1]
    steps = 4
    block = rows // steps

    def body(momentum_hbm, grad_hbm, basis_hbm, high_ref, low_ref, top_ref, bottom_ref, momentum_ref, grad_ref, basis_ref, both_ref, sems):
        whole = pltpu.make_async_copy(basis_hbm, basis_ref, sems.at[0])
        whole.start()
        copies = []
        for i in range(steps):
            at = pl.ds(i * block, block)
            pair = (
                pltpu.make_async_copy(momentum_hbm.at[at], momentum_ref.at[at], sems.at[1 + 2 * i]),
                pltpu.make_async_copy(grad_hbm.at[at], grad_ref.at[at], sems.at[2 + 2 * i]),
            )
            for copy in pair:
                copy.start()
            copies.append(pair)
        whole.wait()
        high, low = split(basis_ref[...])
        both_ref[:, :rank] = high
        both_ref[:, rank:] = low
        for i in range(steps):
            for copy in copies[i]:
                copy.wait()
            at = pl.ds(i * block, block)
            high, low = split(momentum_ref[at, :] + grad_ref[at, :].astype(F32))
            high_ref[at, :] = high
            low_ref[at, :] = low
            wide = dot(high, both_ref[...])
            out_ref = top_ref if 2 * i < steps else bottom_ref
            at = pl.ds(i % (steps // 2) * block, block)
            out_ref[at, :] = wide[:, :rank] + wide[:, rank:] + dot(low, both_ref[:, :rank])

    return pl.pallas_call(
        body,
        in_specs=[pl.BlockSpec(memory_space=pltpu.HBM)] * 3,
        out_specs=[VMEM] * 4,
        out_shape=[struct(rows, cols, dtype=BF16)] * 2 + [struct(rows // 2, rank)] * 2,
        scratch_shapes=[
            pltpu.VMEM((rows, cols), F32),
            pltpu.VMEM((rows, cols), BF16),
            pltpu.VMEM((cols, rank), F32),
            pltpu.VMEM((cols, 2 * rank), BF16),
            pltpu.SemaphoreType.DMA((1 + 2 * steps,)),
        ],
        name="start",
        compiler_params=pltpu.CompilerParams(vmem_limit_bytes=24 * 2**20),
    )(*(pltpu.with_memory_space_constraint(x, pltpu.HBM) for x in (momentum, grad, basis)))


def pull_rows(turned, proj, high_ref, low_ref, cross, right_ref, out_ref):
    half = turned.shape[0]
    width = high_ref.shape[1]
    high, low = split(turned)
    both = jnp.concatenate([high, low], axis=0)
    for at, size in tiles(width):
        wide = dot(both, high_ref[:, at:at + size])
        out = wide[:half] + wide[half:] + dot(high, low_ref[:, at:at + size])
        if cross is not None:
            right_high, right_low = split(right_ref[:, at:at + size])
            wide = dot(jnp.concatenate(cross, axis=0), right_high)
            out = out + (wide[:half] + wide[half:] + dot(cross[0], right_low))
        out_ref[:, at:at + size] = out
    return gram_rows(high, low, both, proj)


def gram_rows(high, low, both, proj):
    half, rank = high.shape[0], proj.shape[1]
    proj_high, proj_low = split(proj)
    wide = dot(both, jnp.concatenate([proj_high, proj_low], axis=1))
    return wide[:half, :rank] + wide[:half, rank:] + wide[half:, :rank]


def put_gram(place, gram, out_ref, width, chunk):
    for t in range(gram.shape[0] // chunk):
        at = pl.multiple_of((place // 2 ^ t) * chunk, chunk)
        out_ref[pl.ds(at, chunk), width:] = gram[t * chunk:(t + 1) * chunk]


def pull_send(count, place, halves, high, low, before=None):
    rows, width = high.shape
    rank = halves[0].shape[1]
    chunk = rank // count

    pairs = len(halves)

    def body(place_ref, *rest):
        place = place_ref[0]
        sums = [one[...] + two[...] for one, two in zip(rest[0:pairs:2], rest[1:pairs:2])]
        proj = jnp.concatenate(sums, axis=0)
        high_ref, low_ref, *rest = rest[pairs:]
        left_ref = right_ref = None
        if before is not None:
            left_ref, right_ref, gram_ref, inv_ref = rest[:4]
            proj = proj - KEEP * parts3(left_ref[...], gram_ref[...])
            proj = parts3(proj, inv_ref[...], NT)
        proj_ref, keep_ref, send_ref, turned_ref = rest[-4:]
        proj_ref[...] = proj
        turned_ref[...] = proj.T

        def pick(other):
            at = [chunk_at(place, t, other) * chunk for t in range(count // 2)]
            return jnp.concatenate([turned_ref[pl.ds(pl.multiple_of(x, chunk), chunk), :] for x in at], axis=0)

        keep_ref[...] = pick(False)
        turned = pick(True)
        cross = None if before is None else split(-KEEP * parts3(turned, left_ref[...]))
        gram = pull_rows(turned, proj, high_ref, low_ref, cross, right_ref, send_ref)
        put_gram(place, gram, send_ref, width, chunk)

    out = [struct(rows, rank), struct(rank // 2, rows), struct(rank // 2, width + rank)]
    ins = [place, *halves, high, low] + list(before or [])
    return call(body, "pull_send", out, ins, [pltpu.VMEM((rank, rows), F32)], flops=500_000_000, nbytes=5_000_000)


def pull_keep(count, place, turned, proj, high, low, before=None):
    rows, width = high.shape
    rank = proj.shape[1]
    chunk = rank // count

    def body(place_ref, turned_ref, proj_ref, high_ref, low_ref, *rest):
        place = place_ref[0]
        turned = turned_ref[...]
        cross = right_ref = None
        if before is not None:
            left_ref, right_ref = rest[:2]
            cross = split(-KEEP * parts3(turned, left_ref[...]))
        gram = pull_rows(turned, proj_ref[...], high_ref, low_ref, cross, right_ref, rest[-1])
        put_gram(place, gram, rest[-1], width, chunk)

    ins = [place, turned, proj, high, low] + list(before or [])[:2]
    return call(body, "pull_keep", struct(rank // 2, width + rank), ins, flops=500_000_000, nbytes=5_000_000)


def normal(count, place, inv, own, other):
    rank = inv.shape[0]
    width = own[0].shape[1]
    chunk = rank // count

    def body(place_ref, inv_ref, *rest):
        pieces = rest[:count]
        right_ref, gram_ref, raw_ref = rest[count:]
        place = place_ref[0]
        for i, piece in enumerate(pieces):
            at = chunk_at(place, i % (count // 2), i >= count // 2) * chunk
            raw_ref[pl.ds(pl.multiple_of(at, chunk), chunk), :] = piece[...]
        inv_high, inv_low = split(inv_ref[...])
        inv_both = jnp.concatenate([inv_high, inv_low], axis=0)
        gram = jnp.zeros((rank, rank), F32)
        for at, size in tiles(width):
            raw_high, raw_low = split(raw_ref[:, at:at + size])
            wide = dot(inv_both, raw_high)
            right = wide[:rank] + wide[rank:] + dot(inv_high, raw_low)
            right_ref[:, at:at + size] = right
            high, low = split(right)
            wide = dot(jnp.concatenate([high, low], axis=0), high, NT)
            gram = gram + (wide[:rank] + wide[rank:] + dot(high, low, NT))
        gram_ref[...] = gram

    return call(body, "normal", [struct(rank, width), struct(rank, rank)], [place, inv, *own, *other],
                [pltpu.VMEM((rank, width), F32)], flops=500_000_000, nbytes=2_000_000)


def push(high, low, right):
    rows, width = high.shape
    rank = right.shape[0]

    def body(high_ref, low_ref, right_ref, out_ref):
        image = None
        for at, size in tiles(width):
            right_high, right_low = split(right_ref[:, at:at + size])
            wide = dot(high_ref[:, at:at + size], jnp.concatenate([right_high, right_low], axis=0), NT)
            part = wide[:, :rank] + wide[:, rank:] + dot(low_ref[:, at:at + size], right_high, NT)
            image = part if image is None else image + part
        out_ref[...] = image

    return call(body, "push", struct(rows, rank), [high, low, right], flops=1_000_000_000, nbytes=5_000_000)


def left_of(proj, inv, before=None, scale=None):
    def body(proj_ref, inv_ref, *rest):
        left = parts3(proj_ref[...], inv_ref[...], NT)
        if before is None:
            rest[0][...] = left
        else:
            before_ref, left_ref, both_ref = rest
            left_ref[...] = left
            both_ref[0] = scale * before_ref[...]
            both_ref[1] = scale * left

    rows, rank = proj.shape
    if before is None:
        return call(body, "left", struct(rows, rank), [proj, inv], flops=100_000_000, nbytes=600_000)
    return call(body, "lefts", [struct(rows, rank), struct(2, rows, rank)], [proj, inv, before],
                flops=100_000_000, nbytes=1_200_000)


def outer_tile(left, right_high, right_low):
    high, low = split(left)
    rows = left.shape[0]
    wide = dot(jnp.concatenate([high, low], axis=0), right_high)
    return wide[:rows] + wide[rows:] + dot(high, right_low)


def deflate(momentum, grad, left, right):
    rows, cols = momentum.shape
    block = rows // 4

    def body(momentum_ref, grad_ref, left_ref, right_ref, out_ref):
        for at, size in tiles(cols):
            lanes = slice(at, at + size)
            right_high, right_low = split(KEEP * right_ref[:, lanes])
            for i in range(4):
                row = slice(i * block, (i + 1) * block)
                work = momentum_ref[row, lanes] + grad_ref[row, lanes].astype(F32)
                out_ref[row, lanes] = work - outer_tile(left_ref[row, :], right_high, right_low)

    return call(body, "deflate", struct(rows, cols), [momentum, grad, left, right], flops=1_500_000_000, nbytes=9_000_000)


def finish(base, left, right, before=None):
    rows, cols = base.shape
    rank = left.shape[1]
    half = rows // 2
    block = half // 2
    first = 0 if before is None else half

    def body(base_ref, left_ref, right_ref, *rest):
        out_ref, stage_ref, high_ref, low_ref, sems = rest[-5:]
        for at, size in tiles(cols):
            lanes = slice(at, at + size)
            high_ref[:, lanes], low_ref[:, lanes] = split(KEEP * right_ref[:, lanes])
        copies = []
        for i in range(2):
            row = slice(first + i * block, first + (i + 1) * block)
            for at, size in tiles(cols):
                lanes = slice(at, at + size)
                outer = outer_tile(left_ref[row, :], high_ref[:, lanes], low_ref[:, lanes])
                stage_ref[i, :, lanes] = base_ref[row, lanes] - outer
            copy = pltpu.make_async_copy(stage_ref.at[i], out_ref.at[pl.ds(first + i * block, block)], sems.at[i])
            copy.start()
            copies.append(copy)
        for copy in copies:
            copy.wait()

    hbm = pl.BlockSpec(memory_space=pltpu.HBM)
    more = [] if before is None else [before]
    return pl.pallas_call(
        body,
        in_specs=[VMEM] * 3 + [hbm] * len(more),
        out_specs=hbm,
        out_shape=struct(rows, cols),
        scratch_shapes=[pltpu.VMEM((2, block, cols), F32)] + [pltpu.VMEM((rank, cols), BF16)] * 2
        + [pltpu.SemaphoreType.DMA((2,))],
        input_output_aliases={3: 0} if more else {},
        name="finish",
        compiler_params=pltpu.CompilerParams(vmem_limit_bytes=24 * 2**20),
        cost_estimate=pl.CostEstimate(flops=800_000_000, bytes_accessed=6_000_000, transcendentals=0),
    )(base, left, right, *more)


def eliminate(full, first, size):
    rank = full.shape[1]
    groups = size // 8
    sub = lax.broadcasted_iota(jnp.int32, (8, rank), 0)
    lane = lax.broadcasted_iota(jnp.int32, (8, rank), 1)
    rolled = pltpu.roll(full, lax.rem(rank - first, rank), 1)
    rows = [full[8 * g:8 * g + 8] for g in range(groups)]
    cols = [
        [jnp.broadcast_to(rolled[8 * g:8 * g + 8, j:j + 1], (8, rank)) for g in range(groups)] for j in range(size)
    ]

    def spread(x, j):
        return jnp.broadcast_to(x[j // 8][j % 8:j % 8 + 1], (8, rank))

    pivot = spread(cols[0], 0)
    for j in range(size):
        at = j // 8
        root = lax.rsqrt(pivot)
        if j + 1 < size:
            above = spread(cols[j + 1], j) * root
            pivot = spread(cols[j + 1], j + 1) - above * above
        below = sub > j % 8
        here = lane == first + j
        row = jnp.where(here, 1.0, spread(rows, j)) * root
        for g in range(at, groups):
            mult = cols[j][g] * root
            rest = jnp.where(here, 0.0, rows[g])
            if g == at:
                mult = jnp.where(below, mult, 0.0)
                rest = jnp.where(below, rest, rows[g])
            rest = rest - mult * row
            rows[g] = jnp.where(sub == j % 8, row, rest) if g == at else rest
            cols[j][g] = mult
        for k in range(j + 1, size):
            across = spread(cols[k], j) * root
            for g in range(at, groups):
                cols[k][g] = cols[k][g] - cols[j][g] * across
    return jnp.concatenate(rows, axis=0)


def thirds(x):
    high = x.astype(BF16)
    rest = x - high.astype(F32)
    middle = rest.astype(BF16)
    return high, middle, (rest - middle.astype(F32)).astype(BF16)


def factor_panels(state_ref, size=PANEL):
    rank = state_ref.shape[0]
    row = lax.broadcasted_iota(jnp.int32, (rank, rank), 0)
    col = lax.broadcasted_iota(jnp.int32, (rank, rank), 1)
    sub = lax.broadcasted_iota(jnp.int32, (size, rank), 0)
    lane = lax.broadcasted_iota(jnp.int32, (size, rank), 1)

    def panel(p, carry):
        first = pl.multiple_of(p * size, size)
        done = eliminate(state_ref[pl.ds(first, size), :], first, size)
        lower = jnp.where((lane > first + sub) & (lane < first + size), 0.0, done)
        a, b, c = thirds(done)
        d, e, f = thirds(lower)
        step = dot(
            jnp.concatenate([a, a, b, b, a, c], axis=0), jnp.concatenate([d, e, d, e, f, d], axis=0), TN
        )
        old = state_ref[...]
        fresh = jnp.where((col >= first) & (col < first + size), 0.0, old) - step
        state_ref[...] = jnp.where(row >= first + size, fresh, old)
        state_ref[pl.ds(first, size), :] = done
        return carry

    lax.fori_loop(0, rank // size - 1, panel, 0)
    state_ref[rank - size:, :] = eliminate(state_ref[rank - size:, :], rank - size, size)


def factor_left(count, place, own, other):
    chunk, rank = own.shape[0], 2 * own.shape[1] // count

    def body(place_ref, own_ref, other_ref, out_ref):
        core = place_ref[0] % 2
        for t in range(count // 2):
            for ref, at in ((own_ref, 2 * t + core), (other_ref, 2 * t + 1 - core)):
                out_ref[pl.ds(pl.multiple_of(at * chunk, chunk), chunk), :] = ref[:, t * rank:(t + 1) * rank]
        factor_panels(out_ref)
        out_ref[...] = lower_part(out_ref[...])

    return call(body, "factor", struct(rank, rank), [place, own, other], flops=2 * FACTOR, nbytes=131072)


def tree_sum(xs):
    while len(xs) > 1:
        xs = [x + y for x, y in zip(xs[::2], xs[1::2])]
    return xs[0]


def factor_right(grams):
    rank = grams[0].shape[0]

    def body(*refs):
        gram_ref, out_ref = refs[-2:]
        gram = tree_sum([ref[...] for ref in refs[:-2]])
        gram_ref[...] = gram
        out_ref[...] = gram
        factor_panels(out_ref)
        out_ref[...] = lower_part(out_ref[...])

    return call(body, "factor", [struct(rank, rank)] * 2, grams, flops=2 * FACTOR, nbytes=131072)


def lower_part(x):
    row = lax.broadcasted_iota(jnp.int32, x.shape, 0)
    col = lax.broadcasted_iota(jnp.int32, x.shape, 1)
    return jnp.where(row >= col, x, 0.0)


def turn(right):
    rank, width = right.shape

    def body(right_ref, high_ref, low_ref):
        high, low = split(right_ref[...].T)
        high_ref[...] = high
        low_ref[...] = low

    return call(body, "turn", [struct(width, rank, dtype=BF16)] * 2, [right], flops=100_000_000, nbytes=2_000_000)


def last_factor(grams, high, low, scale):
    width, rank = high.shape
    steps = 4
    block = width // steps

    def body(high_ref, low_ref, *rest):
        out_ref, state_ref, stage_ref, sems = rest[-4:]
        state_ref[...] = tree_sum([ref[...] for ref in rest[:-4]])
        factor_panels(state_ref)
        inv_high, inv_low = split(scale * lower_part(state_ref[...]))
        both = jnp.concatenate([inv_high, inv_low], axis=0)
        copies = []
        for i in range(steps):
            row = slice(i * block, (i + 1) * block)
            wide = dot(high_ref[row, :], both, NT)
            stage_ref[row, :] = wide[:, :rank] + wide[:, rank:] + dot(low_ref[row, :], inv_high, NT)
            at = pl.ds(i * block, block)
            copy = pltpu.make_async_copy(stage_ref.at[at], out_ref.at[at], sems.at[i])
            copy.start()
            copies.append(copy)
        for copy in copies:
            copy.wait()

    return pl.pallas_call(
        body,
        in_specs=[VMEM] * (2 + len(grams)),
        out_specs=pl.BlockSpec(memory_space=pltpu.HBM),
        out_shape=struct(width, rank),
        scratch_shapes=[pltpu.VMEM((rank, rank), F32), pltpu.VMEM((width, rank), F32), pltpu.SemaphoreType.DMA((steps,))],
        name="last_factor",
        compiler_params=pltpu.CompilerParams(vmem_limit_bytes=24 * 2**20),
        cost_estimate=pl.CostEstimate(flops=2 * FACTOR, bytes_accessed=2_000_000, transcendentals=0),
    )(high, low, *grams)


def sum_cols(parts):
    masks = masks_of("col")
    for even, odd in zip(masks[:-1], masks[:0:-1]):
        parts = [x + swap(x, "col", even, odd) for x in parts]
    return [y for x in parts for y in (x, swap(x, "col", masks[-1], masks[0]))]


def share_cols(x):
    return [x] + [swap(x, "col", mask, mask) for mask in range(1, lax.axis_size("col"))]


def sum_rows(keep, send, count, rank, beside=None):
    x = keep + swap(send, "row", 1, 1)
    if beside is not None:
        work, seed = beside
        x, seed = lax.optimization_barrier((x, seed))
        beside = work(seed)
    width = x.shape[1] - rank
    chunk = rank // count
    slots = count // 2
    cut = width // rank // 2 * rank
    cut = width - cut
    parts = [x[i * chunk:(i + 1) * chunk] for i in range(slots)]
    gram = jnp.concatenate([part[:, width:] for part in parts], axis=1)
    stepped = {i: part[:, cut:width] for i, part in enumerate(parts)}
    own = parts[0][:, :cut]
    straight = {}
    bit = 1
    while bit < slots:
        sent = [i for i in stepped if i & bit]
        kept = [i for i in stepped if not i & bit]
        cols = [stepped[i] for i in sent] + [gram]
        first = [parts[1][:, :cut]] if bit == 1 else []
        got = swap(jnp.concatenate(first + cols, axis=1), "row", 2 * bit, 2 * bit)
        if bit == 1:
            straight[1], got = got[:, :cut], got[:, cut:]
            for i in reversed(range(2, slots)):
                straight[i] = swap(parts[i][:, :cut], "row", 2 * i, 2 * i)
            if beside is not None:
                got, beside = lax.optimization_barrier((got, beside))
        size = width - cut
        stepped = {i: stepped[i] + got[:, n * size:(n + 1) * size] for n, i in enumerate(kept)}
        gram = gram + got[:, len(kept) * size:]
        bit *= 2
    for i in straight:
        own = own + straight[i]
    own = jnp.concatenate([own, stepped[0]], axis=1)
    own, gram = lax.optimization_barrier((own, gram))
    return own, gram, swap(gram, "row", 1, 1), beside


def gather_rows(x, count, meanwhile):
    own = [x] + [swap(x, "row", 2 * i, 2 * i) for i in range(1, count // 2)]
    done = meanwhile()
    other = [swap(x, "row", 1, 1)]
    for piece in own[1:]:
        piece, done = lax.optimization_barrier((piece, done))
        other.append(swap(piece, "row", 1, 1))
    return own, other, done


def shards(momentum, grad, basis):
    count = lax.axis_size("row")
    rank = basis.shape[1]
    rows, width = momentum.shape
    row_scale = float(rows * count) ** 0.5
    col_scale = float(width * lax.axis_size("col")) ** 0.5
    place = lax.axis_index("row").astype(jnp.int32).reshape(1)

    def left_side(halves, before=None, beside=None):
        proj, turned, send = pull_send(count, place, halves, high, low, before)
        keep = pull_keep(count, place, turned, proj, high, low, before)
        raw, own, other, beside = sum_rows(keep, send, count, rank, beside)
        first, second, inv = gather_rows(raw, count, lambda: factor_left(count, place, own, other))
        return proj, inv, (first, second), beside

    high, low, *parts = start(momentum, grad, basis)
    proj, inv, pieces, _ = left_side(sum_cols(parts))
    left_a = left_of(proj, inv)
    right_a, gram = normal(count, place, inv, *pieces)
    gram, inv = factor_right(share_cols(gram))
    halves = sum_cols([push(high, low, right_a)])

    beside = (lambda left: deflate(momentum, grad, left, right_a)), left_a
    proj, inv, pieces, base = left_side(halves, (left_a, right_a, gram, inv), beside)
    left_b, lefts = left_of(proj, inv, left_a, row_scale)
    right_b, gram = normal(count, place, inv, *pieces)

    grams = share_cols(gram)
    momentum_out = finish(base, left_b, right_b)
    momentum_out = finish(base, left_b, right_b, momentum_out)
    return momentum_out, lefts, last_factor(grams, *turn(right_b), col_scale)


def solution(mesh):
    in_specs = (P("row", "col"), P("row", "col"), P("col", None))
    out_specs = (P("row", "col"), P(None, "row", None), P("col", None))
    return jax.shard_map(shards, mesh=mesh, in_specs=in_specs, out_specs=out_specs, check_vma=False)
```

```python
import jax
import jax.numpy as jnp
from jax import lax
from jax.experimental import pallas as pl
from jax.experimental.pallas import tpu as pltpu
from jax.sharding import PartitionSpec as P

F32 = jnp.float32
BF16 = jnp.bfloat16
HIGHEST = lax.Precision.HIGHEST
VMEM = pl.BlockSpec(memory_space=pltpu.VMEM)
SMEM = pl.BlockSpec(memory_space=pltpu.SMEM)
NN = (((1,), (0,)), ((), ()))
NT = (((1,), (1,)), ((), ()))
TN = (((0,), (0,)), ((), ()))
KEEP = 0.95
PANEL = 16
FACTOR = 20_000_000_000


def masks_of(axis):
    size = lax.axis_size(axis)
    masks = []
    mask = 1
    while mask < size:
        masks.append(mask)
        mask *= 2
    assert mask == size
    return masks


def swap(x, axis, even, odd):
    row_count, col_count = lax.axis_size("row"), lax.axis_size("col")
    pairs = []
    for row in range(row_count):
        mask = odd if row % 2 else even
        for col in range(col_count):
            to = (row ^ mask) * col_count + col if axis == "row" else row * col_count + (col ^ mask)
            pairs.append((row * col_count + col, to))
    return lax.ppermute(x, ("row", "col"), pairs)


def chunk_at(place, slot, other=False):
    return place ^ (2 * slot + (1 if other else 0))


def split(x):
    high = x.astype(BF16)
    return high, (x - high.astype(F32)).astype(BF16)


def dot(a, b, dims=NN):
    return lax.dot_general(a, b, dims, preferred_element_type=F32)


def exact(a, b, dims=NN):
    return lax.dot_general(a, b, dims, precision=HIGHEST, preferred_element_type=F32)


def parts3(a, b, dims=NN):
    a_high, a_low = split(a)
    b_high, b_low = split(b)
    return dot(a_high, b_high, dims) + (dot(a_low, b_high, dims) + dot(a_high, b_low, dims))


def tiles(width, most=256):
    return [(start, min(most, width - start)) for start in range(0, width, most)]


def struct(*shape, dtype=F32):
    return jax.ShapeDtypeStruct(shape, dtype)


def call(body, name, out, ins, scratch=(), flops=0, nbytes=0, **kw):
    return pl.pallas_call(
        body,
        out_shape=out,
        in_specs=[SMEM if x.dtype == jnp.int32 else VMEM for x in ins],
        out_specs=jax.tree.map(lambda _: VMEM, out),
        scratch_shapes=list(scratch),
        name=name,
        compiler_params=pltpu.CompilerParams(vmem_limit_bytes=24 * 2**20),
        cost_estimate=pl.CostEstimate(flops=flops, bytes_accessed=nbytes, transcendentals=0),
        **kw,
    )(*ins)


def start(momentum, grad, basis):
    rows, cols = momentum.shape
    rank = basis.shape[1]
    steps = 4
    block = rows // steps

    def body(momentum_hbm, grad_hbm, basis_hbm, high_ref, low_ref, top_ref, bottom_ref, momentum_ref, grad_ref, basis_ref, both_ref, sems):
        whole = pltpu.make_async_copy(basis_hbm, basis_ref, sems.at[0])
        whole.start()
        copies = []
        for i in range(steps):
            at = pl.ds(i * block, block)
            pair = (
                pltpu.make_async_copy(momentum_hbm.at[at], momentum_ref.at[at], sems.at[1 + 2 * i]),
                pltpu.make_async_copy(grad_hbm.at[at], grad_ref.at[at], sems.at[2 + 2 * i]),
            )
            for copy in pair:
                copy.start()
            copies.append(pair)
        whole.wait()
        high, low = split(basis_ref[...])
        both_ref[:, :rank] = high
        both_ref[:, rank:] = low
        for i in range(steps):
            for copy in copies[i]:
                copy.wait()
            at = pl.ds(i * block, block)
            high, low = split(momentum_ref[at, :] + grad_ref[at, :].astype(F32))
            high_ref[at, :] = high
            low_ref[at, :] = low
            wide = dot(high, both_ref[...])
            out_ref = top_ref if 2 * i < steps else bottom_ref
            at = pl.ds(i % (steps // 2) * block, block)
            out_ref[at, :] = wide[:, :rank] + wide[:, rank:] + dot(low, both_ref[:, :rank])

    return pl.pallas_call(
        body,
        in_specs=[pl.BlockSpec(memory_space=pltpu.HBM)] * 3,
        out_specs=[VMEM] * 4,
        out_shape=[struct(rows, cols, dtype=BF16)] * 2 + [struct(rows // 2, rank)] * 2,
        scratch_shapes=[
            pltpu.VMEM((rows, cols), F32),
            pltpu.VMEM((rows, cols), BF16),
            pltpu.VMEM((cols, rank), F32),
            pltpu.VMEM((cols, 2 * rank), BF16),
            pltpu.SemaphoreType.DMA((1 + 2 * steps,)),
        ],
        name="start",
        compiler_params=pltpu.CompilerParams(vmem_limit_bytes=24 * 2**20),
    )(*(pltpu.with_memory_space_constraint(x, pltpu.HBM) for x in (momentum, grad, basis)))


def pull_rows(turned, proj, high_ref, low_ref, cross, right_ref, out_ref):
    half = turned.shape[0]
    width = high_ref.shape[1]
    high, low = split(turned)
    both = jnp.concatenate([high, low], axis=0)
    for at, size in tiles(width):
        wide = dot(both, high_ref[:, at:at + size])
        out = wide[:half] + wide[half:] + dot(high, low_ref[:, at:at + size])
        if cross is not None:
            right_high, right_low = split(right_ref[:, at:at + size])
            wide = dot(jnp.concatenate(cross, axis=0), right_high)
            out = out + (wide[:half] + wide[half:] + dot(cross[0], right_low))
        out_ref[:, at:at + size] = out
    return gram_rows(high, low, both, proj)


def gram_rows(high, low, both, proj):
    half, rank = high.shape[0], proj.shape[1]
    proj_high, proj_low = split(proj)
    wide = dot(both, jnp.concatenate([proj_high, proj_low], axis=1))
    return wide[:half, :rank] + wide[:half, rank:] + wide[half:, :rank]


def put_gram(place, gram, out_ref, width, chunk):
    for t in range(gram.shape[0] // chunk):
        at = pl.multiple_of((place // 2 ^ t) * chunk, chunk)
        out_ref[pl.ds(at, chunk), width:] = gram[t * chunk:(t + 1) * chunk]


def pull_send(count, place, halves, high, low, before=None):
    rows, width = high.shape
    rank = halves[0].shape[1]
    chunk = rank // count

    pairs = len(halves)

    def body(place_ref, *rest):
        place = place_ref[0]
        sums = [one[...] + two[...] for one, two in zip(rest[0:pairs:2], rest[1:pairs:2])]
        proj = jnp.concatenate(sums, axis=0)
        high_ref, low_ref, *rest = rest[pairs:]
        left_ref = right_ref = None
        if before is not None:
            left_ref, right_ref, gram_ref, inv_ref = rest[:4]
            proj = proj - KEEP * parts3(left_ref[...], gram_ref[...])
            proj = parts3(proj, inv_ref[...], NT)
        proj_ref, keep_ref, send_ref, turned_ref = rest[-4:]
        proj_ref[...] = proj
        turned_ref[...] = proj.T

        def pick(other):
            at = [chunk_at(place, t, other) * chunk for t in range(count // 2)]
            return jnp.concatenate([turned_ref[pl.ds(pl.multiple_of(x, chunk), chunk), :] for x in at], axis=0)

        keep_ref[...] = pick(False)
        turned = pick(True)
        cross = None if before is None else split(-KEEP * parts3(turned, left_ref[...]))
        gram = pull_rows(turned, proj, high_ref, low_ref, cross, right_ref, send_ref)
        put_gram(place, gram, send_ref, width, chunk)

    out = [struct(rows, rank), struct(rank // 2, rows), struct(rank // 2, width + rank)]
    ins = [place, *halves, high, low] + list(before or [])
    return call(body, "pull_send", out, ins, [pltpu.VMEM((rank, rows), F32)], flops=500_000_000, nbytes=5_000_000)


def pull_keep(count, place, turned, proj, high, low, before=None):
    rows, width = high.shape
    rank = proj.shape[1]
    chunk = rank // count

    def body(place_ref, turned_ref, proj_ref, high_ref, low_ref, *rest):
        place = place_ref[0]
        turned = turned_ref[...]
        cross = right_ref = None
        if before is not None:
            left_ref, right_ref = rest[:2]
            cross = split(-KEEP * parts3(turned, left_ref[...]))
        gram = pull_rows(turned, proj_ref[...], high_ref, low_ref, cross, right_ref, rest[-1])
        put_gram(place, gram, rest[-1], width, chunk)

    ins = [place, turned, proj, high, low] + list(before or [])[:2]
    return call(body, "pull_keep", struct(rank // 2, width + rank), ins, flops=500_000_000, nbytes=5_000_000)


def normal(count, place, inv, own, other):
    rank = inv.shape[0]
    width = own[0].shape[1]
    chunk = rank // count

    def body(place_ref, inv_ref, *rest):
        pieces = rest[:count]
        right_ref, gram_ref, raw_ref = rest[count:]
        place = place_ref[0]
        for i, piece in enumerate(pieces):
            at = chunk_at(place, i % (count // 2), i >= count // 2) * chunk
            raw_ref[pl.ds(pl.multiple_of(at, chunk), chunk), :] = piece[...]
        inv_high, inv_low = split(inv_ref[...])
        inv_both = jnp.concatenate([inv_high, inv_low], axis=0)
        gram = jnp.zeros((rank, rank), F32)
        for at, size in tiles(width):
            raw_high, raw_low = split(raw_ref[:, at:at + size])
            wide = dot(inv_both, raw_high)
            right = wide[:rank] + wide[rank:] + dot(inv_high, raw_low)
            right_ref[:, at:at + size] = right
            high, low = split(right)
            wide = dot(jnp.concatenate([high, low], axis=0), high, NT)
            gram = gram + (wide[:rank] + wide[rank:] + dot(high, low, NT))
        gram_ref[...] = gram

    return call(body, "normal", [struct(rank, width), struct(rank, rank)], [place, inv, *own, *other],
                [pltpu.VMEM((rank, width), F32)], flops=500_000_000, nbytes=2_000_000)


def push(high, low, right):
    rows, width = high.shape
    rank = right.shape[0]

    def body(high_ref, low_ref, right_ref, out_ref):
        image = None
        for at, size in tiles(width):
            right_high, right_low = split(right_ref[:, at:at + size])
            wide = dot(high_ref[:, at:at + size], jnp.concatenate([right_high, right_low], axis=0), NT)
            part = wide[:, :rank] + wide[:, rank:] + dot(low_ref[:, at:at + size], right_high, NT)
            image = part if image is None else image + part
        out_ref[...] = image

    return call(body, "push", struct(rows, rank), [high, low, right], flops=1_000_000_000, nbytes=5_000_000)


def left_of(proj, inv, before=None, scale=None):
    def body(proj_ref, inv_ref, *rest):
        left = parts3(proj_ref[...], inv_ref[...], NT)
        if before is None:
            rest[0][...] = left
        else:
            before_ref, left_ref, both_ref = rest
            left_ref[...] = left
            both_ref[0] = scale * before_ref[...]
            both_ref[1] = scale * left

    rows, rank = proj.shape
    if before is None:
        return call(body, "left", struct(rows, rank), [proj, inv], flops=100_000_000, nbytes=600_000)
    return call(body, "lefts", [struct(rows, rank), struct(2, rows, rank)], [proj, inv, before],
                flops=100_000_000, nbytes=1_200_000)


def outer_tile(left, right_high, right_low):
    high, low = split(left)
    rows = left.shape[0]
    wide = dot(jnp.concatenate([high, low], axis=0), right_high)
    return wide[:rows] + wide[rows:] + dot(high, right_low)


def deflate(momentum, grad, left, right):
    rows, cols = momentum.shape
    block = rows // 4

    def body(momentum_ref, grad_ref, left_ref, right_ref, out_ref):
        for at, size in tiles(cols):
            lanes = slice(at, at + size)
            right_high, right_low = split(KEEP * right_ref[:, lanes])
            for i in range(4):
                row = slice(i * block, (i + 1) * block)
                work = momentum_ref[row, lanes] + grad_ref[row, lanes].astype(F32)
                out_ref[row, lanes] = work - outer_tile(left_ref[row, :], right_high, right_low)

    return call(body, "deflate", struct(rows, cols), [momentum, grad, left, right], flops=1_500_000_000, nbytes=9_000_000)


def finish(base, left, right, before=None):
    rows, cols = base.shape
    rank = left.shape[1]
    half = rows // 2
    block = half // 2
    first = 0 if before is None else half

    def body(base_ref, left_ref, right_ref, *rest):
        out_ref, stage_ref, high_ref, low_ref, sems = rest[-5:]
        for at, size in tiles(cols):
            lanes = slice(at, at + size)
            high_ref[:, lanes], low_ref[:, lanes] = split(KEEP * right_ref[:, lanes])
        copies = []
        for i in range(2):
            row = slice(first + i * block, first + (i + 1) * block)
            for at, size in tiles(cols):
                lanes = slice(at, at + size)
                outer = outer_tile(left_ref[row, :], high_ref[:, lanes], low_ref[:, lanes])
                stage_ref[i, :, lanes] = base_ref[row, lanes] - outer
            copy = pltpu.make_async_copy(stage_ref.at[i], out_ref.at[pl.ds(first + i * block, block)], sems.at[i])
            copy.start()
            copies.append(copy)
        for copy in copies:
            copy.wait()

    hbm = pl.BlockSpec(memory_space=pltpu.HBM)
    more = [] if before is None else [before]
    return pl.pallas_call(
        body,
        in_specs=[VMEM] * 3 + [hbm] * len(more),
        out_specs=hbm,
        out_shape=struct(rows, cols),
        scratch_shapes=[pltpu.VMEM((2, block, cols), F32)] + [pltpu.VMEM((rank, cols), BF16)] * 2
        + [pltpu.SemaphoreType.DMA((2,))],
        input_output_aliases={3: 0} if more else {},
        name="finish",
        compiler_params=pltpu.CompilerParams(vmem_limit_bytes=24 * 2**20),
        cost_estimate=pl.CostEstimate(flops=800_000_000, bytes_accessed=6_000_000, transcendentals=0),
    )(base, left, right, *more)


def eliminate(full, first, size):
    rank = full.shape[1]
    groups = size // 8
    sub = lax.broadcasted_iota(jnp.int32, (8, rank), 0)
    lane = lax.broadcasted_iota(jnp.int32, (8, rank), 1)
    rolled = pltpu.roll(full, lax.rem(rank - first, rank), 1) if not isinstance(first, int) else full[:, first:first + size]
    rows = [full[8 * g:8 * g + 8] for g in range(groups)]
    cols = [
        [jnp.broadcast_to(rolled[8 * g:8 * g + 8, j:j + 1], (8, rank)) for g in range(groups)] for j in range(size)
    ]

    def spread(x, j):
        return jnp.broadcast_to(x[j // 8][j % 8:j % 8 + 1], (8, rank))

    pivot = spread(cols[0], 0)
    for j in range(size):
        at = j // 8
        root = lax.rsqrt(pivot)
        if j + 1 < size:
            above = spread(cols[j + 1], j) * root
            pivot = spread(cols[j + 1], j + 1) - above * above
        below = sub > j % 8
        here = lane == first + j
        row = jnp.where(here, 1.0, spread(rows, j)) * root
        for g in range(at, groups):
            mult = cols[j][g] * root
            rest = jnp.where(here, 0.0, rows[g])
            if g == at:
                mult = jnp.where(below, mult, 0.0)
                rest = jnp.where(below, rest, rows[g])
            rest = rest - mult * row
            rows[g] = jnp.where(sub == j % 8, row, rest) if g == at else rest
            cols[j][g] = mult
        for k in range(j + 1, size):
            across = spread(cols[k], j) * root
            for g in range(at, groups):
                cols[k][g] = cols[k][g] - cols[j][g] * across
    return jnp.concatenate(rows, axis=0)


def thirds(x):
    high = x.astype(BF16)
    rest = x - high.astype(F32)
    middle = rest.astype(BF16)
    return high, middle, (rest - middle.astype(F32)).astype(BF16)


def factor_panels(state_ref, size=PANEL):
    rank = state_ref.shape[0]
    row = lax.broadcasted_iota(jnp.int32, (rank, rank), 0)
    col = lax.broadcasted_iota(jnp.int32, (rank, rank), 1)
    sub = lax.broadcasted_iota(jnp.int32, (size, rank), 0)
    lane = lax.broadcasted_iota(jnp.int32, (size, rank), 1)

    def panel(p, carry):
        first = pl.multiple_of(p * size, size)
        done = eliminate(state_ref[pl.ds(first, size), :], first, size)
        lower = jnp.where((lane > first + sub) & (lane < first + size), 0.0, done)
        a, b, c = thirds(done)
        d, e, f = thirds(lower)
        step = dot(
            jnp.concatenate([a, a, b, b, a, c], axis=0), jnp.concatenate([d, e, d, e, f, d], axis=0), TN
        )
        old = state_ref[...]
        fresh = jnp.where((col >= first) & (col < first + size), 0.0, old) - step
        state_ref[...] = jnp.where(row >= first + size, fresh, old)
        state_ref[pl.ds(first, size), :] = done
        return carry

    lax.fori_loop(0, rank // size - 1, panel, 0)
    state_ref[rank - size:, :] = eliminate(state_ref[rank - size:, :], rank - size, size)


def factor_unrolled(state_ref):
    rank = state_ref.shape[0]
    sub = lax.broadcasted_iota(jnp.int32, (PANEL, rank), 0)
    lane = lax.broadcasted_iota(jnp.int32, (PANEL, rank), 1)
    for first in range(0, rank, PANEL):
        last = first + PANEL
        done = eliminate(state_ref[first:last, :], first, PANEL)
        state_ref[first:last, :] = done
        if last == rank:
            break
        lower = jnp.where((lane > first + sub) & (lane < last), 0.0, done)
        a, b, c = thirds(done)
        d, e, f = thirds(lower)
        step = dot(
            jnp.concatenate([a, a, b, b, a, c], axis=0), jnp.concatenate([d, e, d, e, f, d], axis=0), TN
        )
        inside = (lane >= first) & (lane < last)
        for row in range(last, rank, PANEL):
            old = state_ref[row:row + PANEL, :]
            state_ref[row:row + PANEL, :] = jnp.where(inside, 0.0, old) - step[row:row + PANEL, :]


def factor_left(count, place, own, other):
    chunk, rank = own.shape[0], 2 * own.shape[1] // count

    def body(place_ref, own_ref, other_ref, out_ref):
        core = place_ref[0] % 2
        for t in range(count // 2):
            for ref, at in ((own_ref, 2 * t + core), (other_ref, 2 * t + 1 - core)):
                out_ref[pl.ds(pl.multiple_of(at * chunk, chunk), chunk), :] = ref[:, t * rank:(t + 1) * rank]
        factor_panels(out_ref)
        out_ref[...] = lower_part(out_ref[...])

    return call(body, "factor", struct(rank, rank), [place, own, other], flops=2 * FACTOR, nbytes=131072)


def tree_sum(xs):
    while len(xs) > 1:
        xs = [x + y for x, y in zip(xs[::2], xs[1::2])]
    return xs[0]


def factor_right(grams):
    rank = grams[0].shape[0]

    def body(*refs):
        gram_ref, out_ref = refs[-2:]
        gram = tree_sum([ref[...] for ref in refs[:-2]])
        gram_ref[...] = gram
        out_ref[...] = gram
        factor_unrolled(out_ref)
        out_ref[...] = lower_part(out_ref[...])

    return call(body, "factor", [struct(rank, rank)] * 2, grams, flops=2 * FACTOR, nbytes=131072)


def lower_part(x):
    row = lax.broadcasted_iota(jnp.int32, x.shape, 0)
    col = lax.broadcasted_iota(jnp.int32, x.shape, 1)
    return jnp.where(row >= col, x, 0.0)


def turn(right):
    rank, width = right.shape

    def body(right_ref, high_ref, low_ref):
        high, low = split(right_ref[...].T)
        high_ref[...] = high
        low_ref[...] = low

    return call(body, "turn", [struct(width, rank, dtype=BF16)] * 2, [right], flops=100_000_000, nbytes=2_000_000)


def last_factor(grams, high, low, scale):
    width, rank = high.shape
    steps = 4
    block = width // steps

    def body(high_ref, low_ref, *rest):
        out_ref, state_ref, stage_ref, sems = rest[-4:]
        state_ref[...] = tree_sum([ref[...] for ref in rest[:-4]])
        factor_unrolled(state_ref)
        inv_high, inv_low = split(scale * lower_part(state_ref[...]))
        both = jnp.concatenate([inv_high, inv_low], axis=0)
        copies = []
        for i in range(steps):
            row = slice(i * block, (i + 1) * block)
            wide = dot(high_ref[row, :], both, NT)
            stage_ref[row, :] = wide[:, :rank] + wide[:, rank:] + dot(low_ref[row, :], inv_high, NT)
            at = pl.ds(i * block, block)
            copy = pltpu.make_async_copy(stage_ref.at[at], out_ref.at[at], sems.at[i])
            copy.start()
            copies.append(copy)
        for copy in copies:
            copy.wait()

    return pl.pallas_call(
        body,
        in_specs=[VMEM] * (2 + len(grams)),
        out_specs=pl.BlockSpec(memory_space=pltpu.HBM),
        out_shape=struct(width, rank),
        scratch_shapes=[pltpu.VMEM((rank, rank), F32), pltpu.VMEM((width, rank), F32), pltpu.SemaphoreType.DMA((steps,))],
        name="last_factor",
        compiler_params=pltpu.CompilerParams(vmem_limit_bytes=24 * 2**20),
        cost_estimate=pl.CostEstimate(flops=2 * FACTOR, bytes_accessed=2_000_000, transcendentals=0),
    )(high, low, *grams)


def sum_cols(parts):
    masks = masks_of("col")
    for even, odd in zip(masks[:-1], masks[:0:-1]):
        parts = [x + swap(x, "col", even, odd) for x in parts]
    return [y for x in parts for y in (x, swap(x, "col", masks[-1], masks[0]))]


def share_cols(x):
    others = [swap(x, "col", mask, mask) for mask in reversed(range(1, lax.axis_size("col")))]
    return [x] + others[::-1]


def sum_rows(keep, send, count, rank, beside=None):
    x = keep + swap(send, "row", 1, 1)
    if beside is not None:
        work, seed = beside
        x, seed = lax.optimization_barrier((x, seed))
        beside = work(seed)
    width = x.shape[1] - rank
    chunk = rank // count
    slots = count // 2
    cut = width // rank // 2 * rank
    cut = width - cut
    parts = [x[i * chunk:(i + 1) * chunk] for i in range(slots)]
    gram = jnp.concatenate([part[:, width:] for part in parts], axis=1)
    stepped = {i: part[:, cut:width] for i, part in enumerate(parts)}
    own = parts[0][:, :cut]
    straight = {}
    bit = 1
    while bit < slots:
        sent = [i for i in stepped if i & bit]
        kept = [i for i in stepped if not i & bit]
        cols = [stepped[i] for i in sent] + [gram]
        first = [parts[1][:, :cut]] if bit == 1 else []
        got = swap(jnp.concatenate(first + cols, axis=1), "row", 2 * bit, 2 * bit)
        if bit == 1:
            straight[1], got = got[:, :cut], got[:, cut:]
            for i in reversed(range(2, slots)):
                straight[i] = swap(parts[i][:, :cut], "row", 2 * i, 2 * i)
            if beside is not None:
                got, beside = lax.optimization_barrier((got, beside))
        size = width - cut
        stepped = {i: stepped[i] + got[:, n * size:(n + 1) * size] for n, i in enumerate(kept)}
        gram = gram + got[:, len(kept) * size:]
        bit *= 2
    for i in straight:
        own = own + straight[i]
    own = jnp.concatenate([own, stepped[0]], axis=1)
    own, gram = lax.optimization_barrier((own, gram))
    return own, gram, swap(gram, "row", 1, 1), beside


def gather_rows(x, count, meanwhile):
    own = [x] + [swap(x, "row", 2 * i, 2 * i) for i in range(1, count // 2)]
    done = meanwhile()
    other = [swap(x, "row", 1, 1)]
    for piece in own[1:]:
        piece, done = lax.optimization_barrier((piece, done))
        other.append(swap(piece, "row", 1, 1))
    return own, other, done


def shards(momentum, grad, basis):
    count = lax.axis_size("row")
    rank = basis.shape[1]
    rows, width = momentum.shape
    row_scale = float(rows * count) ** 0.5
    col_scale = float(width * lax.axis_size("col")) ** 0.5
    place = lax.axis_index("row").astype(jnp.int32).reshape(1)

    def left_side(halves, before=None, beside=None):
        proj, turned, send = pull_send(count, place, halves, high, low, before)
        keep = pull_keep(count, place, turned, proj, high, low, before)
        raw, own, other, beside = sum_rows(keep, send, count, rank, beside)
        first, second, inv = gather_rows(raw, count, lambda: factor_left(count, place, own, other))
        return proj, inv, (first, second), beside

    high, low, *parts = start(momentum, grad, basis)
    proj, inv, pieces, _ = left_side(sum_cols(parts))
    left_a = left_of(proj, inv)
    right_a, gram = normal(count, place, inv, *pieces)
    gram, inv = factor_right(share_cols(gram))
    halves = sum_cols([push(high, low, right_a)])

    beside = (lambda left: deflate(momentum, grad, left, right_a)), left_a
    proj, inv, pieces, base = left_side(halves, (left_a, right_a, gram, inv), beside)
    left_b, lefts = left_of(proj, inv, left_a, row_scale)
    right_b, gram = normal(count, place, inv, *pieces)

    grams = share_cols(gram)
    momentum_out = finish(base, left_b, right_b)
    momentum_out = finish(base, left_b, right_b, momentum_out)
    return momentum_out, lefts, last_factor(grams, *turn(right_b), col_scale)


def solution(mesh):
    in_specs = (P("row", "col"), P("row", "col"), P("col", None))
    out_specs = (P("row", "col"), P(None, "row", None), P("col", None))
    return jax.shard_map(shards, mesh=mesh, in_specs=in_specs, out_specs=out_specs, check_vma=False)
```
